1024 devices in a mesh: dom: 64 (over z, y), inner: 16 (over x, core).
Axes of the slice: x: 8, y: 8, z: 8, core: 2. Of those that a mesh axis runs over, the one named last changes fastest.
Arguments:
- leaf_multipoles: float32 [8, 64, 524288], P(None, None, ('dom', 'inner')), may hold values from -6 to 6
- m2m_ops: float32 [8, 64, 64], replicated, may hold values from -0.25 to 0.25
- l2l_ops: float32 [8, 64, 64], replicated, may hold values from -0.75 to 0.75
- m2l_ops: float32 [189, 64, 64], replicated, may hold values from -0.0625 to 0.0625
- send_blocks: int32 [64, 16, 4, 2], P('dom', 'inner'), may hold values from 0 to 7, as said below
- send_counts: int32 [64, 16, 4], P('dom', 'inner'), may hold values from 0 to 2, as said below
- list1_src: int32 [64, 16, 8, 120], P('dom', 'inner'), may hold values from 0 to 15, as said below
- list1_pat: int32 [64, 16, 8, 120], P('dom', 'inner'), may hold values from 0 to 188
- list2_src: int32 [64, 16, 1, 8], P('dom', 'inner'), may hold values from 0 to 15
- list2_pat: int32 [64, 16, 1, 8], P('dom', 'inner'), may hold values from 0 to 188
Outputs:
- leaf_locals: float32 [8, 64, 524288], P(None, None, ('dom', 'inner'))
The draws below stay inside these ranges and needn't reach their ends.
Inputs may be any that keep to these rules, and one draw needn't show every extreme that they name: `send_blocks`: entries are local block numbers below 8. `send_counts`: A count is zero where the destination domain d + off(w) lies outside the domains; every sender fills 2 slots for some neighbouring domain, and for every inner index some domain receives 2 blocks from each of its 4 neighbours. `list1_src`: an entry v below 8 names the device's own block v; otherwise v - 8 = w * 2 + c names slot c received from domain d + off(w), which exists, and c is below that sender's count for this device.
All inputs are finite; a program needn't handle non-finite values.
Results may differ from the reference program's by a relative error of at most 0.0003.
Values sent between devices are 32-bit elements; how exact they have to be, the bound alone decides.
No kernel may reach another device: no remote copies, remote signals or barrier semaphores. Data moves between devices by JAX's collectives and lax.ppermute only.
A program may use at most 32 MiB of HBM per device.

```python
import jax
import jax.numpy as jnp
from jax import lax

NCOEF = 64
BLOCK = 64
B2_DEV = 1
NL1 = 120
NL2 = 8
NPAT = 189
CAP = 2
HALF = 2
NWIN = 4
B1_DEV = 8
P1 = 524288
N_DOM = 64
N_INNER = 16


def window_offsets():
    window = jnp.arange(NWIN, dtype=jnp.int32)
    return jnp.where(window < HALF, window - HALF, window - HALF + 1).astype(jnp.int32)


def shared_counts(key):
    key_base, key_favour, key_hottest = jax.random.split(key, 3)
    offsets = window_offsets()
    window = jnp.arange(NWIN, dtype=jnp.int32)[None, None, :]
    domains = jnp.arange(N_DOM, dtype=jnp.int32)[:, None, None]
    destination = domains + offsets[None, None, :]
    valid = (destination >= 0) & (destination < N_DOM)
    drawn_base = jax.random.randint(key_base, (N_DOM, N_INNER, NWIN), 0, CAP + 1)
    favoured = jax.random.randint(key_favour, (N_DOM, N_INNER, 1), 0, NWIN)
    favoured_dest = domains + jnp.take(offsets, favoured)
    favoured_ok = (favoured_dest >= 0) & (favoured_dest < N_DOM)
    favoured = jnp.where(favoured_ok, favoured, NWIN - 1 - favoured)
    filled = jnp.where(window == favoured, CAP, drawn_base)
    hottest = jax.random.randint(key_hottest, (1, N_INNER, 1), HALF, N_DOM - HALF)
    filled = jnp.where(destination == hottest, CAP, filled)
    filled = jnp.where(valid, filled, 0)
    return (filled.astype(jnp.int32), hottest)


def draw_send_counts(key, part):
    filled, hottest = shared_counts(key)
    return filled


def draw_send_blocks(key, part):
    key = jax.random.fold_in(key, 5)
    return jax.random.randint(key, (N_DOM, N_INNER, NWIN, CAP), 0, B1_DEV).astype(jnp.int32)


def draw_list1_src(key, part):
    filled, hottest = shared_counts(key)
    key = jax.random.fold_in(key, 7)
    key_win, key_spread, key_own, key_pick = jax.random.split(key, 4)
    offsets = window_offsets()
    window = jnp.arange(NWIN, dtype=jnp.int32)
    domains = jnp.arange(N_DOM, dtype=jnp.int32)[:, None]
    source_dom = domains + offsets[None, :]
    valid = (source_dom >= 0) & (source_dom < N_DOM)
    clipped = jnp.clip(source_dom, 0, N_DOM - 1)
    mirror = jnp.broadcast_to((NWIN - 1 - window)[None, :], (N_DOM, NWIN))
    receive = filled[clipped, :, mirror]
    receive = jnp.where(valid[:, :, None], receive, 0)
    receive = jnp.transpose(receive, (0, 2, 1))
    shape = (N_DOM, N_INNER, B1_DEV * NL1)
    source_win = jax.random.randint(key_win, shape, 0, NWIN)
    available = jnp.take_along_axis(receive, source_win, axis=2)
    spread = jax.random.randint(key_spread, shape, 0, 1 << 20)
    slot_index = spread % jnp.maximum(available, 1)
    remote = B1_DEV + source_win * CAP + slot_index
    own_pick = jax.random.randint(key_own, shape, 0, B1_DEV)
    remote_pick = jax.random.randint(key_pick, shape, 0, 2)
    chosen = jnp.where((remote_pick == 1) & (available > 0), remote, own_pick)
    chosen = chosen.reshape(N_DOM, N_INNER, B1_DEV, NL1)
    highest = B1_DEV + NWIN * CAP - 1
    chosen = chosen.at[hottest[0, 0, 0], 0, 0, 0].set(highest)
    return chosen.astype(jnp.int32)


def with_ends(entries, key, least, largest):
    longest = entries.shape.index(max(entries.shape))
    spots = []
    for shift in (0, 1):
        where = [jax.random.randint(jax.random.fold_in(key, axis), (), 0, length) for axis, length in enumerate(entries.shape)]
        where[longest] = (where[longest] + shift) % entries.shape[longest]
        spots.append(tuple(where))
    return entries.at[spots[0]].set(least).at[spots[1]].set(largest)


def steps_of(stream_key, extent, shards, smallest, top_value):
    def one(dim, shards_of):
        draws = jax.random.uniform(jax.random.fold_in(jax.random.fold_in(stream_key, 6), dim), (shards_of,), jnp.float32, smallest / len(shards), top_value / len(shards))
        return jnp.repeat(jnp.exp(draws), extent[dim] // shards_of).reshape((-1,) + (1,) * (len(extent) - dim - 1))

    level = one(*shards[0])
    for cut in shards[1:]:
        level = level * one(*cut)
    return level


def centred(stream_key, shape, scale, most, shards=(), kind=jnp.bfloat16):
    result = jax.random.normal(stream_key, shape, jnp.float32) * scale
    if len(shards) > 0:
        result = steps_of(stream_key, shape, shards, -0.22, 0.18) * result
    return jnp.clip(result, min=-most, max=most).astype(kind)


def setup_inputs(seed: int = 0) -> dict:
    key_of = jax.random.split(jax.random.key(seed), 11)
    return {
        "leaf_multipoles": centred(key_of[0], (8, NCOEF, P1), 1.0, 6.0, ((2, 1024),), jnp.float32),
        "m2m_ops": centred(key_of[1], (8, NCOEF, NCOEF), (8 * NCOEF) ** -0.5, 0.25, (), jnp.float32),
        "l2l_ops": centred(key_of[2], (8, NCOEF, NCOEF), NCOEF ** -0.5, 0.75, (), jnp.float32),
        "m2l_ops": centred(key_of[3], (NPAT, NCOEF, NCOEF), (NCOEF * NL1) ** -0.5, 0.0625, (), jnp.float32),
        "send_blocks": draw_send_blocks(jax.random.fold_in(key_of[10], 71), 0),
        "send_counts": draw_send_counts(jax.random.fold_in(key_of[10], 71), 0),
        "list1_src": draw_list1_src(jax.random.fold_in(key_of[10], 71), 0),
        "list1_pat": with_ends(jax.random.randint(key_of[7], (N_DOM, N_INNER, B1_DEV, NL1), 0, NPAT), jax.random.fold_in(key_of[7], 1), 0, NPAT - 1).astype(jnp.int32),
        "list2_src": with_ends(jax.random.randint(key_of[8], (N_DOM, N_INNER, B2_DEV, NL2), 0, N_INNER * B2_DEV), jax.random.fold_in(key_of[8], 1), 0, (N_INNER * B2_DEV) - 1).astype(jnp.int32),
        "list2_pat": with_ends(jax.random.randint(key_of[9], (N_DOM, N_INNER, B2_DEV, NL2), 0, NPAT), jax.random.fold_in(key_of[9], 1), 0, NPAT - 1).astype(jnp.int32),
    }


def reference(leaf_multipoles, m2m_ops, l2l_ops, m2l_ops, send_blocks, send_counts, list1_src, list1_pat, list2_src, list2_pat):
    precise = lax.Precision.HIGHEST
    level1 = jnp.einsum("ock,okp->cp", m2m_ops, leaf_multipoles, precision=precise)
    grouped = level1.reshape(NCOEF, P1 // 8, 8)
    level2 = jnp.einsum("ock,kqo->cq", m2m_ops, grouped, precision=precise)
    blocks_one = level1.reshape(NCOEF, N_DOM, N_INNER, B1_DEV, BLOCK)
    blocks_two = level2.reshape(NCOEF, N_DOM, N_INNER * B2_DEV, BLOCK)
    boxes_dev = BLOCK * B1_DEV
    window = jnp.arange(NWIN, dtype=jnp.int32)
    offsets = jnp.where(window < HALF, window - HALF, window - HALF + 1).astype(jnp.int32)
    mirror = (NWIN - 1 - window).astype(jnp.int32)

    def one_device(device):
        domain_index = device // N_INNER
        inner_index = device % N_INNER
        source_dom = domain_index + offsets
        valid = (source_dom >= 0) & (source_dom < N_DOM)
        clipped = jnp.clip(source_dom, 0, N_DOM - 1).astype(jnp.int32)
        senders = jnp.take(blocks_one, inner_index, axis=2)
        window_senders = jnp.take(senders, clipped, axis=1)
        send_inner = jnp.take(send_blocks, inner_index, axis=1)
        sent_index = send_inner[clipped, mirror]
        counts = jnp.take(send_counts, inner_index, axis=1)[clipped, mirror]
        counts = jnp.where(valid, counts, jnp.zeros((), jnp.int32))
        full_index = jnp.broadcast_to(sent_index[None, :, :, None], (NCOEF, NWIN, CAP, BLOCK))
        arrived = jnp.take_along_axis(window_senders, full_index, axis=2)
        filled = jnp.arange(CAP, dtype=jnp.int32)[None, :] < counts[:, None]
        arrived = jnp.where(filled[None, :, :, None], arrived, jnp.zeros((), arrived.dtype))
        own_blocks = jnp.take(jnp.take(blocks_one, domain_index, axis=1), inner_index, axis=1)
        source_table = jnp.concatenate([own_blocks, arrived.reshape(NCOEF, NWIN * CAP, BLOCK)], axis=1)
        sources = list1_src[domain_index, inner_index]
        patterns = list1_pat[domain_index, inner_index]
        chosen = jnp.take(source_table, sources.reshape(-1), axis=1).reshape(NCOEF, B1_DEV, NL1, BLOCK)
        matrices = jnp.take(m2l_ops, patterns.reshape(-1), axis=0).reshape(B1_DEV, NL1, NCOEF, NCOEF)
        far_first = jnp.einsum("njck,knjb->cnb", matrices, chosen, precision=precise).reshape(NCOEF, boxes_dev)
        domain = jnp.take(blocks_two, domain_index, axis=1)
        sources_two = list2_src[domain_index, inner_index]
        patterns_two = list2_pat[domain_index, inner_index]
        chosen_two = jnp.take(domain, sources_two.reshape(-1), axis=1).reshape(NCOEF, B2_DEV, NL2, BLOCK)
        matrices_two = jnp.take(m2l_ops, patterns_two.reshape(-1), axis=0).reshape(B2_DEV, NL2, NCOEF, NCOEF)
        far_second = jnp.einsum("njck,knjb->cnb", matrices_two, chosen_two, precision=precise).reshape(NCOEF, boxes_dev // 8)
        lowered = jnp.einsum("ock,kq->cqo", l2l_ops, far_second, precision=precise).reshape(NCOEF, boxes_dev)
        local_first = far_first + lowered
        return jnp.einsum("ock,kp->ocp", l2l_ops, local_first, precision=precise)

    results = lax.map(one_device, jnp.arange(N_DOM * N_INNER, dtype=jnp.int32))
    return jnp.transpose(results, (1, 2, 0, 3)).reshape(8, NCOEF, P1)
```

```python
import functools

import jax
import jax.numpy as jnp
from jax import lax
from jax.experimental import pallas as pl
from jax.experimental.pallas import tpu as pltpu
from jax.sharding import PartitionSpec as P

F32 = jnp.float32
BF16 = jnp.bfloat16
NT = (((1,), (1,)), ((), ()))


def split(x):
    high = x.astype(BF16)
    return high, (x - high.astype(F32)).astype(BF16)


def dot(a, b):
    return jnp.dot(a, b, preferred_element_type=F32)


def dot_nt(a, b):
    return lax.dot_general(a, b, NT, preferred_element_type=F32)


def dot3(a, b, product=dot):
    return product(a[0], b[0]) + (product(a[0], b[1]) + product(a[1], b[0]))


def lanes(shape):
    return lax.broadcasted_iota(jnp.int32, shape, len(shape) - 1)


def rows(shape):
    return lax.broadcasted_iota(jnp.int32, shape, len(shape) - 2)


def four_blocks(low, high):
    none = jnp.zeros_like(low)
    left = jnp.concatenate([low, high, none, none], axis=0)
    right = jnp.concatenate([none, none, low, high], axis=0)
    return jnp.concatenate([left, right], axis=1)


def spread(pair):
    first = lanes(pair.shape) < 64
    turned = pltpu.roll(pair, 64, 1)
    result = []
    for side in (0, 1):
        low, high = (pair, turned) if side == 0 else (turned, pair)
        low = split(jnp.where(first, low, 0.0))
        high = split(jnp.where(first, 0.0, high))
        result.append((four_blocks(low[0], high[0]), four_blocks(low[1], high[1])))
    return result


def upward_kernel(blocks_ref, counts_ref, leaf_ref, m2m_ref, level1_ref, sends_ref, level2_ref, ops, turned, grouped, twice):
    for o in range(8):
        ops[:, o * 64 : (o + 1) * 64] = m2m_ref[o]
    operators = split(ops[...])
    leaf = leaf_ref[...].reshape(512, 512)
    level1 = dot3(operators, split(leaf))
    level1_ref[...] = level1
    first = lanes((64, 128)) < 64
    for t in range(4):
        tile = level1[:, t * 128 : (t + 1) * 128]
        other = pltpu.roll(tile, 64, 1)
        twice[2 * t] = jnp.where(first, tile, other)
        twice[2 * t + 1] = jnp.where(first, other, tile)
    for w in range(4):
        count = counts_ref[0, 0, w]
        left = jnp.where(count > 0, twice[blocks_ref[0, 0, w, 0]], 0.0)
        right = jnp.where(count > 1, twice[blocks_ref[0, 0, w, 1]], 0.0)
        sends_ref[w] = jnp.where(first, left, right)
    turned[...] = jnp.concatenate([level1, level1], axis=0).T
    for o in range(8):
        grouped[:, o * 64 : (o + 1) * 64] = turned[pl.ds(o, 64, stride=8), :][:, 0:64]
    level2 = dot3(operators, split(grouped[...]), dot_nt)
    for copy in range(8):
        level2_ref[copy, :, 0:64] = level2[0:32]
        level2_ref[copy, :, 64:128] = level2[32:64]


def weights_kernel(src_ref, pat_ref, pat2_ref, m2l_ref, level1_ref, high_ref, low_ref, own_ref, second_ref, table):
    patterns = m2l_ref.shape[2]
    entries = src_ref.shape[1]
    code = src_ref[...] * 8 + rows((8, entries))
    pat = pat_ref[...]
    tally = jnp.zeros((128, patterns), F32)
    for r in range(8):
        sources = jnp.where(code[r : r + 1] == rows((128, entries)), 1.0, 0.0).astype(BF16)
        kinds = jnp.where(pat[r : r + 1] == rows((patterns, entries)), 1.0, 0.0).astype(BF16)
        tally = tally + dot_nt(sources, kinds)
    single = jnp.where(pat2_ref[...] == lanes((16, patterns)), 1.0, 0.0)
    picks = jnp.concatenate([tally, single], axis=0).astype(BF16)
    for g in range(16):
        high, low = split(jnp.concatenate([m2l_ref[16 * c + g] for c in range(4)], axis=0))
        table[g] = dot_nt(picks, high) + dot_nt(picks, low)
    for s in range(8, 16):
        high, low = split(table[:, 8 * s : 8 * s + 8, :].reshape(128, 256))
        high_ref[s - 8] = high
        low_ref[s - 8] = low
    for h in range(2):
        second_ref[h] = table[:, 128:136, 128 * h : 128 * h + 128].reshape(128, 128)
    total = jnp.zeros((128, 256), F32)
    for t in range(4):
        both = spread(level1_ref[:, t * 128 : (t + 1) * 128])
        for side in (0, 1):
            s = 2 * t + side
            total = total + dot3(split(table[:, 8 * s : 8 * s + 8, :].reshape(128, 256)), both[side])
    own_ref[...] = total


def downward_kernel(
    src2_ref, core_ref, high_ref, low_ref, own_ref, second_ref, up_ref, down_ref, level2_ref, l2l_ref, out_ref,
    total_s, wide_s
):
    core = core_ref[0]
    total = own_ref[...]
    for w, (ref, holder) in enumerate(((up_ref, 1), (up_ref, 0), (down_ref, 0), (down_ref, 1))):
        both = spread(ref[holder, core])
        for side in (0, 1):
            slot = 2 * w + side
            total = total + dot3((high_ref[slot], low_ref[slot]), both[side])
    for h in range(2):
        total_s[h] = total[:, 128 * h : 128 * h + 128]
    far = jnp.zeros((16, 256), F32)
    first = lanes((32, 128)) < 64
    for j in range(8):
        source = src2_ref[0, 0, 0, j]
        packed = level2_ref[source % 2, source // 2]
        turned = pltpu.roll(packed, 64, 1)
        low = split(jnp.where(first, jnp.concatenate([packed, turned], 0).reshape(2, 32, 128), 0.0).reshape(64, 128))
        high = split(jnp.where(first, 0.0, jnp.concatenate([turned, packed], 0).reshape(2, 32, 128)).reshape(64, 128))
        block = (four_blocks(low[0], high[0]), four_blocks(low[1], high[1]))
        operator = jnp.concatenate([second_ref[h, pl.ds(j, 16, stride=8), :] for h in range(2)], axis=1)
        far = far + dot3(split(operator), block)
    far = [far[:, 128 * h : 128 * h + 128] for h in range(2)]
    far = jnp.concatenate([part for f in far for part in (f, pltpu.roll(f, 64, 1))], axis=0)[:, 0:64]
    first = lanes((16, 128)) < 64
    local = []
    for t in range(4):
        parts = []
        for h in range(2):
            a = total_s[h, pl.ds(2 * t, 16, stride=8), :]
            b = total_s[h, pl.ds(2 * t + 1, 16, stride=8), :]
            parts.append(jnp.where(first, a, pltpu.roll(b, 64, 1)))
            parts.append(jnp.where(first, pltpu.roll(a, 64, 1), b))
        local.append(jnp.concatenate(parts, axis=0))
    local = jnp.concatenate(local, axis=1)
    operators = split(l2l_ref[...].reshape(512, 64))
    lowered = dot3(operators, split(far))
    for o in range(8):
        wide_s[:, 64 * o : 64 * o + 64] = lowered[64 * o : 64 * o + 64]
    place = 8 * (rows((512, 512)) % 64) + rows((512, 512)) // 64
    order = jnp.where(place == lanes((512, 512)), 1.0, 0.0).astype(BF16)
    wide = wide_s[...]
    head, tail = split(wide)
    local = local + (dot(head, order) + dot(tail, order))
    out_ref[...] = dot3(operators, split(local)).reshape(8, 64, 512)


def on_device(
    leaf_multipoles, m2m_ops, l2l_ops, m2l_ops, send_blocks, send_counts, list1_src, list1_pat, list2_src, list2_pat
):
    smem = pl.BlockSpec(memory_space=pltpu.SMEM)
    vmem = pl.BlockSpec(memory_space=pltpu.VMEM)
    limit = pltpu.CompilerParams(vmem_limit_bytes=40 * 1024 * 1024)
    level1, sends, level2 = pl.pallas_call(
        upward_kernel,
        out_shape=[
            jax.ShapeDtypeStruct((64, 512), F32),
            jax.ShapeDtypeStruct((4, 64, 128), F32),
            jax.ShapeDtypeStruct((8, 32, 128), F32),
        ],
        in_specs=[smem, smem, vmem, vmem],
        out_specs=[vmem] * 3,
        scratch_shapes=[
            pltpu.VMEM((64, 512), F32),
            pltpu.VMEM((512, 128), F32),
            pltpu.VMEM((64, 512), F32),
            pltpu.VMEM((8, 64, 128), F32),
        ],
        compiler_params=limit,
        name="upward",
    )(send_blocks, send_counts, leaf_multipoles, m2m_ops)

    doms, inners = lax.axis_size("dom"), lax.axis_size("inner")
    core = lax.axis_index("inner") % 2
    cores = [[2 * x, 2 * x + 1] for x in range(inners // 2)]
    chips = [[2 * x + c for x in range(inners // 2)] for c in range(2)]

    def routed(block, side):
        route = []
        for d in range(doms):
            for i in range(inners):
                to = d + side * (1 + i % 2)
                if 0 <= to < doms:
                    route.append((d * inners + i, to * inners + i))
        return lax.ppermute(block, ("dom", "inner"), route)

    def both_cores(block):
        return lax.all_gather(block, "inner", axis=0, axis_index_groups=cores)

    chip_sends = both_cores(sends)
    upper = lax.dynamic_index_in_dim(chip_sends, 2 + core, 1, keepdims=False)
    lower = lax.dynamic_index_in_dim(chip_sends, 1 - core, 1, keepdims=False)
    came_up = routed(upper, 1)
    came_down = routed(lower, -1)
    own_side = lax.all_to_all(level2, "inner", 0, 0, axis_index_groups=chips)
    all_level2 = both_cores(own_side)

    patterns = m2l_ops.shape[0]
    high, low, own, second = pl.pallas_call(
        weights_kernel,
        out_shape=[
            jax.ShapeDtypeStruct((8, 128, 256), BF16),
            jax.ShapeDtypeStruct((8, 128, 256), BF16),
            jax.ShapeDtypeStruct((128, 256), F32),
            jax.ShapeDtypeStruct((2, 128, 128), F32),
        ],
        in_specs=[vmem] * 5,
        out_specs=[vmem] * 4,
        scratch_shapes=[pltpu.VMEM((16, 144, 256), F32)],
        compiler_params=limit,
        name="weights",
    )(
        list1_src[0, 0],
        list1_pat[0, 0],
        jnp.pad(list2_pat.reshape(8, 1), ((0, 8), (0, 0)), constant_values=-1),
        jnp.transpose(m2l_ops, (1, 2, 0)),
        level1,
    )
    up = both_cores(came_up)
    down = both_cores(came_down)
    return pl.pallas_call(
        downward_kernel,
        out_shape=jax.ShapeDtypeStruct((8, 64, 512), F32),
        in_specs=[smem, smem] + [vmem] * 8,
        out_specs=vmem,
        scratch_shapes=[
            pltpu.VMEM((2, 128, 128), F32),
            pltpu.VMEM((64, 512), F32),
        ],
        compiler_params=limit,
        name="downward",
    )(list2_src, core.reshape(1), high, low, own, second, up, down, all_level2, l2l_ops)


def solution(mesh):
    placed = (
        P(None, None, ("dom", "inner")),
        P(),
        P(),
        P(),
        P("dom", "inner", None, None),
        P("dom", "inner", None),
        P("dom", "inner", None, None),
        P("dom", "inner", None, None),
        P("dom", "inner", None, None),
        P("dom", "inner", None, None),
    )
    return jax.shard_map(
        on_device,
        mesh=mesh,
        in_specs=placed,
        out_specs=P(None, None, ("dom", "inner")),
        check_vma=False,
    )
```

```python
import jax
import jax.numpy as jnp
from jax import lax
from jax.experimental import pallas as pl
from jax.experimental.pallas import tpu as pltpu
from jax.sharding import PartitionSpec as P

F32 = jnp.float32
BF16 = jnp.bfloat16
NT = (((1,), (1,)), ((), ()))


def split(x):
    high = x.astype(BF16)
    return high, (x - high.astype(F32)).astype(BF16)


def dot(a, b):
    return jnp.dot(a, b, preferred_element_type=F32)


def dot_nt(a, b):
    return lax.dot_general(a, b, NT, preferred_element_type=F32)


def dot3(a, b, product=dot):
    n = a[0].shape[0]
    both = product(jnp.concatenate(a, axis=0), b[0])
    return both[:n] + (product(a[0], b[1]) + both[n:])


def lanes(shape):
    return lax.broadcasted_iota(jnp.int32, shape, len(shape) - 1)


def rows(shape):
    return lax.broadcasted_iota(jnp.int32, shape, len(shape) - 2)


def four_blocks(low, high):
    none = jnp.zeros_like(low)
    left = jnp.concatenate([low, high, none, none], axis=0)
    right = jnp.concatenate([none, none, low, high], axis=0)
    return jnp.concatenate([left, right], axis=1)


def spread(pair):
    first = lanes(pair.shape) < 64
    turned = pltpu.roll(pair, 64, 1)
    result = []
    for side in (0, 1):
        low, high = (pair, turned) if side == 0 else (turned, pair)
        low = split(jnp.where(first, low, 0.0))
        high = split(jnp.where(first, 0.0, high))
        result.append((four_blocks(low[0], high[0]), four_blocks(low[1], high[1])))
    return result


def upward_kernel(
    blocks_hbm, counts_hbm, leaf_hbm, m2m_hbm, level1_ref, sends_ref, level2_ref,
    blocks, counts, leaf, m2m, ops, turned, grouped, twice, sems
):
    def copy(source, target, k):
        return pltpu.make_async_copy(source, target, sems.at[k])

    first_copies = [
        copy(m2m_hbm, m2m, 0),
        copy(leaf_hbm.at[0:4], leaf.at[0:4], 1),
        copy(leaf_hbm.at[4:8], leaf.at[4:8], 2),
        copy(blocks_hbm, blocks, 3),
        copy(counts_hbm, counts, 4),
    ]
    for c in first_copies:
        c.start()
    first_copies[0].wait()
    for o in range(8):
        ops[:, o * 64 : (o + 1) * 64] = m2m[o]
    operators = split(ops[...])
    level1 = jnp.zeros((64, 512), F32)
    for half in range(2):
        first_copies[1 + half].wait()
        operator = [part[:, 256 * half : 256 * half + 256] for part in operators]
        level1 = level1 + dot3(operator, split(leaf[4 * half : 4 * half + 4].reshape(256, 512)))
    level1_ref[...] = level1
    turned[...] = jnp.concatenate([level1, level1], axis=0).T
    for o in range(8):
        grouped[:, o * 64 : (o + 1) * 64] = turned[pl.ds(o, 64, stride=8), :][:, 0:64]
    level2 = dot3(operators, split(grouped[...]), dot_nt)
    first = lanes((32, 128)) < 64
    wide = jnp.concatenate([level2, level2], axis=1)
    packed = jnp.where(first, wide[0:32], wide[32:64])
    for member in range(16):
        level2_ref[member] = packed
    first = lanes((64, 128)) < 64
    for t in range(4):
        tile = level1[:, t * 128 : (t + 1) * 128]
        other = pltpu.roll(tile, 64, 1)
        twice[2 * t] = jnp.where(first, tile, other)
        twice[2 * t + 1] = jnp.where(first, other, tile)
    first_copies[3].wait()
    first_copies[4].wait()
    for w in range(4):
        count = counts[0, 0, w]
        left = jnp.where(count > 0, twice[blocks[0, 0, 0, w]], 0.0)
        right = jnp.where(count > 1, twice[blocks[0, 0, 1, w]], 0.0)
        sends_ref[w] = jnp.where(first, left, right)


def weights_kernel(
    src_ref, pat_ref, src2_ref, pat2_ref, m2l_hbm, level1_ref, high_ref, low_ref, own_ref, second_ref, table, second_s, m2l_ref, sems
):
    patterns = m2l_ref.shape[2]
    copies = [
        [
            pltpu.make_async_copy(m2l_hbm.at[part], m2l_ref.at[part], sems.at[4 * quarter + c])
            for c in range(4)
            for part in [pl.ds(16 * c + 4 * quarter, 4)]
        ]
        for quarter in range(4)
    ]
    for quarter in copies:
        for c in quarter:
            c.start()
    entries = src_ref.shape[1]
    code = src_ref[...] * 8 + rows((8, entries))
    pat = pat_ref[...]
    tally = jnp.zeros((128, patterns), F32)
    for r in range(8):
        sources = jnp.where(code[r : r + 1] == rows((128, entries)), 1.0, 0.0).astype(BF16)
        kinds = jnp.where(pat[r : r + 1] == rows((patterns, entries)), 1.0, 0.0).astype(BF16)
        tally = tally + dot_nt(sources, kinds)
    entries = src2_ref.shape[1]
    sources = jnp.where(src2_ref[...] == rows((16, entries)), 1.0, 0.0).astype(BF16)
    kinds = jnp.where(pat2_ref[...] == rows((patterns, entries)), 1.0, 0.0).astype(BF16)
    picks = jnp.concatenate([tally, dot_nt(sources, kinds)], axis=0).astype(BF16)
    for g in range(16):
        if g % 4 == 0:
            for c in copies[g // 4]:
                c.wait()
        high, low = split(jnp.concatenate([m2l_ref[16 * c + g] for c in range(4)], axis=0))
        operators = dot_nt(picks, high) + dot_nt(picks, low)
        table[g] = operators[0:128]
        for h in range(2):
            second_s[h, 16 * g : 16 * g + 16, :] = operators[128:144, 128 * h : 128 * h + 128]
    for s in range(8, 16):
        high, low = split(table[:, 8 * s : 8 * s + 8, :].reshape(128, 256))
        high_ref[s - 8] = high
        low_ref[s - 8] = low
    first = lanes((16, 128)) < 64
    for t in range(8):
        parts = []
        for h in range(2):
            a = second_s[h, pl.ds(2 * t, 16, stride=16), :]
            b = second_s[h, pl.ds(2 * t + 1, 16, stride=16), :]
            parts.append(jnp.where(first, a, pltpu.roll(b, 64, 1)))
            parts.append(jnp.where(first, pltpu.roll(a, 64, 1), b))
        second_ref[:, 128 * t : 128 * t + 128] = jnp.concatenate(split(jnp.concatenate(parts, axis=0)), axis=0)
    total = jnp.zeros((128, 256), F32)
    for t in range(4):
        both = spread(level1_ref[:, t * 128 : (t + 1) * 128])
        for side in (0, 1):
            s = 2 * t + side
            total = total + dot3(split(table[:, 8 * s : 8 * s + 8, :].reshape(128, 256)), both[side])
    own_ref[...] = total


def downward_kernel(
    high_ref, low_ref, own_ref, second_ref, came_ref, level2_ref, l2l_ref, out_ref, total_s
):
    total = own_ref[...]
    core = lax.axis_index("inner") % 2
    for w, (holder, place) in enumerate(((1, 0), (0, 0), (0, 2), (1, 2))):
        both = spread(came_ref[holder, place + core])
        for side in (0, 1):
            slot = 2 * w + side
            total = total + dot3((high_ref[slot], low_ref[slot]), both[side])
    for h in range(2):
        total_s[h] = total[:, 128 * h : 128 * h + 128]
    first = lanes((32, 128)) < 64
    sources = []
    for source in range(16):
        packed = level2_ref[source]
        turned = pltpu.roll(packed, 64, 1)
        sources += [jnp.where(first, packed, turned), jnp.where(first, turned, packed)]
    sources = split(jnp.concatenate(sources, axis=0))
    far = dot3((second_ref[0:64], second_ref[64:128]), sources)
    first = lanes((16, 128)) < 64
    local = []
    for t in range(4):
        parts = []
        for h in range(2):
            a = total_s[h, pl.ds(2 * t, 16, stride=8), :]
            b = total_s[h, pl.ds(2 * t + 1, 16, stride=8), :]
            parts.append(jnp.where(first, a, pltpu.roll(b, 64, 1)))
            parts.append(jnp.where(first, pltpu.roll(a, 64, 1), b))
        local.append(jnp.concatenate(parts, axis=0))
    local = jnp.concatenate(local, axis=1)
    operators = split(l2l_ref[...].reshape(512, 64))
    lowered = dot3(operators, split(far))
    first = lanes((64, 128)) < 64
    wide = [jnp.where(first, lowered[128 * t : 128 * t + 64], lowered[128 * t + 64 : 128 * t + 128]) for t in range(4)]
    place = 8 * (rows((512, 512)) % 64) + rows((512, 512)) // 64
    order = jnp.where(place == lanes((512, 512)), 1.0, 0.0).astype(BF16)
    head, tail = split(jnp.concatenate(wide, axis=1))
    local = local + (dot(head, order) + dot(tail, order))
    out_ref[...] = dot3(operators, split(local)).reshape(8, 64, 512)


SMEM = pl.BlockSpec(memory_space=pltpu.SMEM)
VMEM = pl.BlockSpec(memory_space=pltpu.VMEM)
HBM = pl.BlockSpec(memory_space=pltpu.HBM)
LIMIT = pltpu.CompilerParams(vmem_limit_bytes=24 * 1024 * 1024)


def in_hbm(x):
    return pltpu.with_memory_space_constraint(x, pltpu.HBM)


def upward(leaf_multipoles, m2m_ops, send_blocks, send_counts):
    return pl.pallas_call(
        upward_kernel,
        out_shape=[
            jax.ShapeDtypeStruct((64, 512), F32),
            jax.ShapeDtypeStruct((4, 64, 128), F32),
            jax.ShapeDtypeStruct((16, 32, 128), F32),
        ],
        in_specs=[HBM] * 4,
        out_specs=[VMEM] * 3,
        scratch_shapes=[
            pltpu.SMEM((1, 1, 2, 4), jnp.int32),
            pltpu.SMEM((1, 1, 4), jnp.int32),
            pltpu.VMEM((8, 64, 512), F32),
            pltpu.VMEM((8, 64, 64), F32),
            pltpu.VMEM((64, 512), F32),
            pltpu.VMEM((512, 128), F32),
            pltpu.VMEM((64, 512), F32),
            pltpu.VMEM((8, 64, 128), F32),
            pltpu.SemaphoreType.DMA((5,)),
        ],
        compiler_params=LIMIT,
        cost_estimate=pl.CostEstimate(flops=10**9, bytes_accessed=12 * 10**6, transcendentals=0),
        name="upward",
    )(
        in_hbm(jnp.transpose(send_blocks, (0, 1, 3, 2))),
        in_hbm(send_counts),
        in_hbm(leaf_multipoles),
        in_hbm(m2m_ops),
    )


def weights(list1_src, list1_pat, list2_src, list2_pat, m2l_ops, level1):
    patterns = m2l_ops.shape[0]
    return pl.pallas_call(
        weights_kernel,
        out_shape=[
            jax.ShapeDtypeStruct((8, 128, 256), BF16),
            jax.ShapeDtypeStruct((8, 128, 256), BF16),
            jax.ShapeDtypeStruct((128, 256), F32),
            jax.ShapeDtypeStruct((128, 1024), BF16),
        ],
        in_specs=[VMEM] * 4 + [HBM] + [VMEM],
        out_specs=[VMEM] * 4,
        scratch_shapes=[
            pltpu.VMEM((16, 128, 256), F32),
            pltpu.VMEM((2, 256, 128), F32),
            pltpu.VMEM((64, 64, patterns), F32),
            pltpu.SemaphoreType.DMA((16,)),
        ],
        compiler_params=LIMIT,
        name="weights",
    )(
        list1_src[0, 0],
        list1_pat[0, 0],
        list2_src[0, 0],
        list2_pat[0, 0],
        in_hbm(jnp.transpose(m2l_ops, (1, 2, 0))),
        level1,
    )


def downward(high, low, own, second, came, all_level2, l2l_ops):
    return pl.pallas_call(
        downward_kernel,
        out_shape=jax.ShapeDtypeStruct((8, 64, 512), F32),
        in_specs=[VMEM] * 7,
        out_specs=VMEM,
        scratch_shapes=[pltpu.VMEM((2, 128, 128), F32)],
        compiler_params=LIMIT,
        name="downward",
    )(high, low, own, second, came, all_level2, l2l_ops)


def on_device(
    leaf_multipoles, m2m_ops, l2l_ops, m2l_ops, send_blocks, send_counts, list1_src, list1_pat, list2_src, list2_pat
):
    doms, inners = lax.axis_size("dom"), lax.axis_size("inner")
    level1, sends, level2 = upward(leaf_multipoles, m2m_ops, send_blocks, send_counts)
    core = lax.axis_index("inner") % 2
    cores = [[2 * x, 2 * x + 1] for x in range(inners // 2)]

    def routed(block, side):
        route = []
        for d in range(doms):
            for i in range(inners):
                to = d + side * (1 + i % 2)
                if 0 <= to < doms:
                    route.append((d * inners + i, to * inners + i))
        return lax.ppermute(block, ("dom", "inner"), route)

    def both_cores(block):
        return lax.all_gather(block, "inner", axis=0, axis_index_groups=cores)

    all_level2 = lax.all_to_all(level2, "inner", 0, 0)
    chip_sends = both_cores(sends)
    upper = lax.dynamic_index_in_dim(chip_sends, 2 + core, 1, keepdims=False)
    lower = lax.dynamic_index_in_dim(chip_sends, 1 - core, 1, keepdims=False)
    came_up = routed(upper, 1)
    came_down = routed(lower, -1)
    operators = weights(list1_src, list1_pat, list2_src, list2_pat, m2l_ops, level1)
    came = both_cores(jnp.concatenate([came_up, came_down], axis=0))
    return downward(*operators, came, all_level2, l2l_ops)


def solution(mesh):
    placed = (
        P(None, None, ("dom", "inner")),
        P(),
        P(),
        P(),
        P("dom", "inner", None, None),
        P("dom", "inner", None),
        P("dom", "inner", None, None),
        P("dom", "inner", None, None),
        P("dom", "inner", None, None),
        P("dom", "inner", None, None),
    )
    return jax.shard_map(
        on_device,
        mesh=mesh,
        in_specs=placed,
        out_specs=P(None, None, ("dom", "inner")),
        check_vma=False,
    )
```

```python
import jax
import jax.numpy as jnp
from jax import lax
from jax.experimental import pallas as pl
from jax.experimental.pallas import tpu as pltpu
from jax.sharding import PartitionSpec as P

F32 = jnp.float32
BF16 = jnp.bfloat16
NT = (((1,), (1,)), ((), ()))


def split(x):
    high = x.astype(BF16)
    return high, (x - high.astype(F32)).astype(BF16)


def dot(a, b):
    return jnp.dot(a, b, preferred_element_type=F32)


def dot_nt(a, b):
    return lax.dot_general(a, b, NT, preferred_element_type=F32)


def dot3(a, b, product=dot):
    n = a[0].shape[0]
    both = product(jnp.concatenate(a, axis=0), b[0])
    return both[:n] + (product(a[0], b[1]) + both[n:])


def dot3_sum(pairs):
    left = [x for a, _ in pairs for x in (a[0], a[0], a[1])]
    right = [x for _, b in pairs for x in (b[0], b[1], b[0])]
    return dot(jnp.concatenate(left, axis=1), jnp.concatenate(right, axis=0))


def dot3k(a, b):
    return dot3_sum([(a, b)])


def lanes(shape):
    return lax.broadcasted_iota(jnp.int32, shape, len(shape) - 1)


def rows(shape):
    return lax.broadcasted_iota(jnp.int32, shape, len(shape) - 2)


def four_blocks(low, high):
    none = jnp.zeros_like(low)
    left = jnp.concatenate([low, high, none, none], axis=0)
    right = jnp.concatenate([none, none, low, high], axis=0)
    return jnp.concatenate([left, right], axis=1)


def spread(pair):
    first = lanes(pair.shape) < 64
    turned = pltpu.roll(pair, 64, 1)
    result = []
    for side in (0, 1):
        low, high = (pair, turned) if side == 0 else (turned, pair)
        low = split(jnp.where(first, low, 0.0))
        high = split(jnp.where(first, 0.0, high))
        result.append((four_blocks(low[0], high[0]), four_blocks(low[1], high[1])))
    return result


def upward_kernel(
    blocks_hbm, counts_hbm, leaf_hbm, m2m_hbm, level1_ref, sends_ref, level2_ref,
    blocks, counts, leaf, m2m, ops, turned, grouped, twice, sems
):
    def copy(source, target, k):
        return pltpu.make_async_copy(source, target, sems.at[k])

    first_copies = [
        copy(m2m_hbm, m2m, 0),
        copy(leaf_hbm.at[0:4], leaf.at[0:4], 1),
        copy(leaf_hbm.at[4:8], leaf.at[4:8], 2),
        copy(blocks_hbm, blocks, 3),
        copy(counts_hbm, counts, 4),
    ]
    for c in first_copies:
        c.start()
    first_copies[0].wait()
    for o in range(8):
        ops[:, o * 64 : (o + 1) * 64] = m2m[o]
    operators = split(ops[...])
    level1 = jnp.zeros((64, 512), F32)
    for half in range(2):
        first_copies[1 + half].wait()
        operator = [part[:, 256 * half : 256 * half + 256] for part in operators]
        level1 = level1 + dot3(operator, split(leaf[4 * half : 4 * half + 4].reshape(256, 512)))
    level1_ref[...] = level1
    turned[...] = jnp.concatenate([level1, level1], axis=0).T
    for o in range(8):
        grouped[:, o * 64 : (o + 1) * 64] = turned[pl.ds(o, 64, stride=8), :][:, 0:64]
    level2 = dot3(operators, split(grouped[...]), dot_nt)
    first = lanes((32, 128)) < 64
    wide = jnp.concatenate([level2, level2], axis=1)
    packed = jnp.where(first, wide[0:32], wide[32:64])
    for member in range(8):
        level2_ref[member] = packed
    first = lanes((64, 128)) < 64
    for t in range(4):
        tile = level1[:, t * 128 : (t + 1) * 128]
        other = pltpu.roll(tile, 64, 1)
        twice[2 * t] = jnp.where(first, tile, other)
        twice[2 * t + 1] = jnp.where(first, other, tile)
    first_copies[3].wait()
    first_copies[4].wait()
    for w in range(4):
        count = counts[0, 0, w]
        left = jnp.where(count > 0, twice[blocks[0, 0, 0, w]], 0.0)
        right = jnp.where(count > 1, twice[blocks[0, 0, 1, w]], 0.0)
        sends_ref[w] = jnp.where(first, left, right)


def weights_kernel(
    src_ref, pat_ref, src2_ref, pat2_ref, m2l_hbm, level1_ref, high_ref, low_ref, own_ref, second_ref, table, second_s, m2l_ref, sems
):
    patterns = m2l_ref.shape[2]
    copies = [
        [
            pltpu.make_async_copy(m2l_hbm.at[part], m2l_ref.at[part], sems.at[4 * quarter + c])
            for c in range(4)
            for part in [pl.ds(16 * c + 4 * quarter, 4)]
        ]
        for quarter in range(4)
    ]
    for quarter in copies:
        for c in quarter:
            c.start()
    entries = src_ref.shape[1]
    code = src_ref[...] * 8 + rows((8, entries))
    pat = pat_ref[...]
    tally = jnp.zeros((128, patterns), F32)
    for r in range(8):
        sources = jnp.where(code[r : r + 1] == rows((128, entries)), 1.0, 0.0).astype(BF16)
        kinds = jnp.where(pat[r : r + 1] == rows((patterns, entries)), 1.0, 0.0).astype(BF16)
        tally = tally + dot_nt(sources, kinds)
    entries = src2_ref.shape[1]
    sources = jnp.where(src2_ref[...] == rows((16, entries)), 1.0, 0.0).astype(BF16)
    kinds = jnp.where(pat2_ref[...] == rows((patterns, entries)), 1.0, 0.0).astype(BF16)
    picks = jnp.concatenate([tally, dot_nt(sources, kinds)], axis=0).astype(BF16)
    for g in range(16):
        if g % 4 == 0:
            for c in copies[g // 4]:
                c.wait()
        high, low = split(jnp.concatenate([m2l_ref[16 * c + g] for c in range(4)], axis=0))
        operators = dot_nt(picks, high) + dot_nt(picks, low)
        table[g] = operators[0:128]
        for h in range(2):
            second_s[h, 16 * g : 16 * g + 16, :] = operators[128:144, 128 * h : 128 * h + 128]
    for s in range(8, 16):
        high, low = split(table[:, 8 * s : 8 * s + 8, :].reshape(128, 256))
        high_ref[s - 8] = high
        low_ref[s - 8] = low
    first = lanes((16, 128)) < 64
    for t in range(8):
        parts = []
        for h in range(2):
            a = second_s[h, pl.ds(2 * t, 16, stride=16), :]
            b = second_s[h, pl.ds(2 * t + 1, 16, stride=16), :]
            parts.append(jnp.where(first, a, pltpu.roll(b, 64, 1)))
            parts.append(jnp.where(first, pltpu.roll(a, 64, 1), b))
        second_ref[:, 128 * t : 128 * t + 128] = jnp.concatenate(split(jnp.concatenate(parts, axis=0)), axis=0)
    total = jnp.zeros((128, 256), F32)
    for t in range(4):
        both = spread(level1_ref[:, t * 128 : (t + 1) * 128])
        for side in (0, 1):
            s = 2 * t + side
            total = total + dot3(split(table[:, 8 * s : 8 * s + 8, :].reshape(128, 256)), both[side])
    own_ref[...] = total


def downward_kernel(
    high_ref, low_ref, own_ref, second_ref, came_ref, l2l_ref, out_ref, total_s
):
    pairs = []
    core = lax.axis_index("inner") % 2
    for w, (holder, place) in enumerate(((1, 0), (0, 0), (0, 2), (1, 2))):
        both = spread(came_ref[holder, place + core])
        for side in (0, 1):
            slot = 2 * w + side
            pairs.append(((high_ref[slot], low_ref[slot]), both[side]))

    total = own_ref[...] + dot3_sum(pairs)
    for h in range(2):
        total_s[h] = total[:, 128 * h : 128 * h + 128]
    first = lanes((32, 128)) < 64
    sources = []
    for source in range(16):
        chip = source // 2
        packed = came_ref[source % 2, 4 + chip // 2, 32 * (chip % 2) : 32 * (chip % 2) + 32, :]
        turned = pltpu.roll(packed, 64, 1)
        sources += [jnp.where(first, packed, turned), jnp.where(first, turned, packed)]
    sources = split(jnp.concatenate(sources, axis=0))
    far = dot3k((second_ref[0:64], second_ref[64:128]), sources)
    first = lanes((16, 128)) < 64
    local = []
    for t in range(4):
        parts = []
        for h in range(2):
            a = total_s[h, pl.ds(2 * t, 16, stride=8), :]
            b = total_s[h, pl.ds(2 * t + 1, 16, stride=8), :]
            parts.append(jnp.where(first, a, pltpu.roll(b, 64, 1)))
            parts.append(jnp.where(first, pltpu.roll(a, 64, 1), b))
        local.append(jnp.concatenate(parts, axis=0))
    local = jnp.concatenate(local, axis=1)
    operators = split(l2l_ref[...].reshape(512, 64))
    lowered = dot3k(operators, split(far))
    first = lanes((64, 128)) < 64
    wide = [jnp.where(first, lowered[128 * t : 128 * t + 64], lowered[128 * t + 64 : 128 * t + 128]) for t in range(4)]
    place = 8 * (rows((512, 512)) % 64) + rows((512, 512)) // 64
    order = jnp.where(place == lanes((512, 512)), 1.0, 0.0).astype(BF16)
    head, tail = split(jnp.concatenate(wide, axis=1))
    local = local + dot(jnp.concatenate([head, tail], axis=1), jnp.concatenate([order, order], axis=0))
    out_ref[...] = dot3k(operators, split(local)).reshape(8, 64, 512)


SMEM = pl.BlockSpec(memory_space=pltpu.SMEM)
VMEM = pl.BlockSpec(memory_space=pltpu.VMEM)
HBM = pl.BlockSpec(memory_space=pltpu.HBM)
LIMIT = pltpu.CompilerParams(vmem_limit_bytes=24 * 1024 * 1024)


def in_hbm(x):
    return pltpu.with_memory_space_constraint(x, pltpu.HBM)


def upward(leaf_multipoles, m2m_ops, send_blocks, send_counts):
    return pl.pallas_call(
        upward_kernel,
        out_shape=[
            jax.ShapeDtypeStruct((64, 512), F32),
            jax.ShapeDtypeStruct((4, 64, 128), F32),
            jax.ShapeDtypeStruct((8, 32, 128), F32),
        ],
        in_specs=[HBM] * 4,
        out_specs=[VMEM] * 3,
        scratch_shapes=[
            pltpu.SMEM((1, 1, 2, 4), jnp.int32),
            pltpu.SMEM((1, 1, 4), jnp.int32),
            pltpu.VMEM((8, 64, 512), F32),
            pltpu.VMEM((8, 64, 64), F32),
            pltpu.VMEM((64, 512), F32),
            pltpu.VMEM((512, 128), F32),
            pltpu.VMEM((64, 512), F32),
            pltpu.VMEM((8, 64, 128), F32),
            pltpu.SemaphoreType.DMA((5,)),
        ],
        compiler_params=LIMIT,
        cost_estimate=pl.CostEstimate(flops=10**9, bytes_accessed=12 * 10**6, transcendentals=0),
        name="upward",
    )(
        in_hbm(jnp.transpose(send_blocks, (0, 1, 3, 2))),
        in_hbm(send_counts),
        in_hbm(leaf_multipoles),
        in_hbm(m2m_ops),
    )


def weights(list1_src, list1_pat, list2_src, list2_pat, m2l_ops, level1):
    patterns = m2l_ops.shape[0]
    return pl.pallas_call(
        weights_kernel,
        out_shape=[
            jax.ShapeDtypeStruct((8, 128, 256), BF16),
            jax.ShapeDtypeStruct((8, 128, 256), BF16),
            jax.ShapeDtypeStruct((128, 256), F32),
            jax.ShapeDtypeStruct((128, 1024), BF16),
        ],
        in_specs=[VMEM] * 4 + [HBM] + [VMEM],
        out_specs=[VMEM] * 4,
        scratch_shapes=[
            pltpu.VMEM((16, 128, 256), F32),
            pltpu.VMEM((2, 256, 128), F32),
            pltpu.VMEM((64, 64, patterns), F32),
            pltpu.SemaphoreType.DMA((16,)),
        ],
        compiler_params=LIMIT,
        name="weights",
    )(
        list1_src[0, 0],
        list1_pat[0, 0],
        list2_src[0, 0],
        list2_pat[0, 0],
        in_hbm(jnp.transpose(m2l_ops, (1, 2, 0))),
        level1,
    )


def downward(high, low, own, second, came, l2l_ops):
    return pl.pallas_call(
        downward_kernel,
        out_shape=jax.ShapeDtypeStruct((8, 64, 512), F32),
        in_specs=[VMEM] * 6,
        out_specs=VMEM,
        scratch_shapes=[pltpu.VMEM((2, 128, 128), F32)],
        compiler_params=LIMIT,
        name="downward",
    )(high, low, own, second, came, l2l_ops)


def on_device(
    leaf_multipoles, m2m_ops, l2l_ops, m2l_ops, send_blocks, send_counts, list1_src, list1_pat, list2_src, list2_pat
):
    doms, inners = lax.axis_size("dom"), lax.axis_size("inner")
    level1, sends, level2 = upward(leaf_multipoles, m2m_ops, send_blocks, send_counts)
    core = lax.axis_index("inner") % 2
    cores = [[2 * x, 2 * x + 1] for x in range(inners // 2)]

    def routed(block, side):
        route = []
        for d in range(doms):
            for i in range(inners):
                to = d + side * (1 + i % 2)
                if 0 <= to < doms:
                    route.append((d * inners + i, to * inners + i))
        return lax.ppermute(block, ("dom", "inner"), route)

    def both_cores(block):
        return lax.all_gather(block, "inner", axis=0, axis_index_groups=cores)

    chips = [[2 * x + c for x in range(inners // 2)] for c in range(2)]
    own_side = lax.all_to_all(level2, "inner", 0, 0, axis_index_groups=chips)
    chip_sends = both_cores(sends)
    upper = lax.dynamic_index_in_dim(chip_sends, 2 + core, 1, keepdims=False)
    lower = lax.dynamic_index_in_dim(chip_sends, 1 - core, 1, keepdims=False)
    came_up = routed(upper, 1)
    came_down = routed(lower, -1)
    operators = weights(list1_src, list1_pat, list2_src, list2_pat, m2l_ops, level1)
    came = jnp.concatenate([came_up, came_down, own_side.reshape(4, 64, 128)], axis=0)
    return downward(*operators, both_cores(came), l2l_ops)


def solution(mesh):
    placed = (
        P(None, None, ("dom", "inner")),
        P(),
        P(),
        P(),
        P("dom", "inner", None, None),
        P("dom", "inner", None),
        P("dom", "inner", None, None),
        P("dom", "inner", None, None),
        P("dom", "inner", None, None),
        P("dom", "inner", None, None),
    )
    return jax.shard_map(
        on_device,
        mesh=mesh,
        in_specs=placed,
        out_specs=P(None, None, ("dom", "inner")),
        check_vma=False,
    )
```

```python
import jax
import jax.numpy as jnp
from jax import lax
from jax.experimental import pallas as pl
from jax.experimental.pallas import tpu as pltpu
from jax.sharding import PartitionSpec as P

F32 = jnp.float32
BF16 = jnp.bfloat16
NT = (((1,), (1,)), ((), ()))


def split(x):
    high = x.astype(BF16)
    return high, (x - high.astype(F32)).astype(BF16)


def dot(a, b):
    return jnp.dot(a, b, preferred_element_type=F32)


def dot_nt(a, b):
    return lax.dot_general(a, b, NT, preferred_element_type=F32)


def dot3(a, b, product=dot):
    n = a[0].shape[0]
    both = product(jnp.concatenate(a, axis=0), b[0])
    return both[:n] + (product(a[0], b[1]) + both[n:])


def dot3_sum(pairs):
    left = [x for a, _ in pairs for x in (a[0], a[0], a[1])]
    right = [x for _, b in pairs for x in (b[0], b[1], b[0])]
    return dot(jnp.concatenate(left, axis=1), jnp.concatenate(right, axis=0))


def dot3k(a, b):
    return dot3_sum([(a, b)])


def lanes(shape):
    return lax.broadcasted_iota(jnp.int32, shape, len(shape) - 1)


def rows(shape):
    return lax.broadcasted_iota(jnp.int32, shape, len(shape) - 2)


def four_blocks(low, high):
    none = jnp.zeros_like(low)
    left = jnp.concatenate([low, high, none, none], axis=0)
    right = jnp.concatenate([none, none, low, high], axis=0)
    return jnp.concatenate([left, right], axis=1)


def spread(pair):
    first = lanes(pair.shape) < 64
    turned = pltpu.roll(pair, 64, 1)
    result = []
    for side in (0, 1):
        low, high = (pair, turned) if side == 0 else (turned, pair)
        low = split(jnp.where(first, low, 0.0))
        high = split(jnp.where(first, 0.0, high))
        result.append((four_blocks(low[0], high[0]), four_blocks(low[1], high[1])))
    return result


EARLY = 8


def translate(picks, m2l_ref, table_ref, second_ref):
    for g in range(m2l_ref.shape[0] // 4):
        high, low = split(m2l_ref[4 * g : 4 * g + 4].reshape(256, m2l_ref.shape[2]))
        operators = dot_nt(jnp.concatenate([picks, picks], axis=1), jnp.concatenate([high, low], axis=1))
        table_ref[g] = operators[0:128]
        for h in range(2):
            second_ref[h, 16 * g : 16 * g + 16, :] = operators[128:144, 128 * h : 128 * h + 128]


def upward_kernel(
    blocks_hbm, counts_hbm, leaf_hbm, m2m_hbm, src_hbm, pat_hbm, src2_hbm, pat2_hbm, m2l_hbm,
    level1_ref, sends_ref, level2_hbm, picks_ref, table_ref, second_ref,
    blocks, counts, leaf, m2m, src_ref, pat_ref, src2_ref, pat2_ref, m2l_ref, ops, turned, grouped, twice, copies, sems
):
    def copy(source, target, k):
        return pltpu.make_async_copy(source, target, sems.at[k])

    first_copies = [
        copy(m2m_hbm, m2m, 0),
        copy(leaf_hbm.at[0:4], leaf.at[0:4], 1),
        copy(leaf_hbm.at[4:8], leaf.at[4:8], 2),
        copy(blocks_hbm, blocks, 3),
        copy(counts_hbm, counts, 4),
    ]
    list_copies = [
        copy(src_hbm, src_ref, 5), copy(pat_hbm, pat_ref, 6), copy(src2_hbm, src2_ref, 7), copy(pat2_hbm, pat2_ref, 8)
    ]
    m2l_copy = copy(m2l_hbm.at[0 : 4 * EARLY], m2l_ref, 10)
    for c in first_copies + list_copies + [m2l_copy]:
        c.start()
    first_copies[0].wait()
    for o in range(8):
        ops[:, o * 64 : (o + 1) * 64] = m2m[o]
    operators = split(ops[...])
    level1 = jnp.zeros((64, 512), F32)
    for half in range(2):
        first_copies[1 + half].wait()
        operator = [part[:, 256 * half : 256 * half + 256] for part in operators]
        level1 = level1 + dot3(operator, split(leaf[4 * half : 4 * half + 4].reshape(256, 512)))
    level1_ref[...] = level1
    turned[...] = jnp.concatenate([level1, level1], axis=0).T
    for o in range(8):
        grouped[:, o * 64 : (o + 1) * 64] = turned[pl.ds(o, 64, stride=8), :][:, 0:64]
    level2 = dot3(operators, split(grouped[...]), dot_nt)
    first = lanes((32, 128)) < 64
    wide = jnp.concatenate([level2, level2], axis=1)
    packed = jnp.where(first, wide[0:32], wide[32:64])
    for member in range(8):
        copies[member] = packed
    level2_copy = copy(copies, level2_hbm, 9)
    level2_copy.start()
    first = lanes((64, 128)) < 64
    for t in range(4):
        tile = level1[:, t * 128 : (t + 1) * 128]
        other = pltpu.roll(tile, 64, 1)
        twice[2 * t] = jnp.where(first, tile, other)
        twice[2 * t + 1] = jnp.where(first, other, tile)
    first_copies[3].wait()
    first_copies[4].wait()
    for w in range(4):
        count = counts[0, 0, w]
        left = jnp.where(count > 0, twice[blocks[0, 0, 0, w]], 0.0)
        right = jnp.where(count > 1, twice[blocks[0, 0, 1, w]], 0.0)
        sends_ref[w] = jnp.where(first, left, right)
    for c in list_copies:
        c.wait()
    patterns = m2l_ref.shape[2]
    entries = src_ref.shape[1]
    code = src_ref[...] * 8 + rows((8, entries))
    pat = pat_ref[...]
    tally = jnp.zeros((128, patterns), F32)
    for r in range(8):
        sources = jnp.where(code[r : r + 1] == rows((128, entries)), 1.0, 0.0).astype(BF16)
        kinds = jnp.where(pat[r : r + 1] == rows((patterns, entries)), 1.0, 0.0).astype(BF16)
        tally = tally + dot_nt(sources, kinds)
    entries = src2_ref.shape[1]
    sources = jnp.where(src2_ref[...] == rows((16, entries)), 1.0, 0.0).astype(BF16)
    kinds = jnp.where(pat2_ref[...] == rows((patterns, entries)), 1.0, 0.0).astype(BF16)
    picks = jnp.concatenate([tally, dot_nt(sources, kinds)], axis=0).astype(BF16)
    picks_ref[...] = picks
    m2l_copy.wait()
    translate(picks, m2l_ref, table_ref, second_ref)
    level2_copy.wait()


def weights_kernel(
    picks_ref, table_ref, early_ref, m2l_hbm, level1_ref, high_ref, low_ref, own_ref, second_ref,
    table, second_s, m2l_ref, sem
):
    m2l_copy = pltpu.make_async_copy(m2l_hbm.at[4 * EARLY : 64], m2l_ref, sem)
    m2l_copy.start()
    m2l_copy.wait()
    translate(picks_ref[...], m2l_ref, table, second_s)

    def operators(s):
        place = pl.ds(8 * s, 8)
        return split(jnp.concatenate([table_ref[:, place, :], table[:, place, :]], axis=0).reshape(128, 256))

    for s in range(8, 16):
        high_ref[s - 8], low_ref[s - 8] = operators(s)
    first = lanes((16, 128)) < 64
    for t in range(8):
        parts = []
        for h in range(2):
            a, b = (
                jnp.concatenate([ref[h, pl.ds(s, ref.shape[1] // 16, stride=16), :] for ref in (early_ref, second_s)], axis=0)
                for s in (2 * t, 2 * t + 1)
            )
            parts.append(jnp.where(first, a, pltpu.roll(b, 64, 1)))
            parts.append(jnp.where(first, pltpu.roll(a, 64, 1), b))
        second_ref[:, 128 * t : 128 * t + 128] = jnp.concatenate(split(jnp.concatenate(parts, axis=0)), axis=0)
    total = jnp.zeros((128, 256), F32)
    for t in range(4):
        both = spread(level1_ref[:, t * 128 : (t + 1) * 128])
        for side in (0, 1):
            total = total + dot3(operators(2 * t + side), both[side])
    own_ref[...] = total


def downward_kernel(
    high_ref, low_ref, own_ref, second_ref, came_ref, l2l_ref, out_ref, total_s, local_s, far_s
):
    pairs = []
    core = lax.axis_index("inner") % 2
    for w, (holder, place) in enumerate(((1, 2), (0, 2), (0, 0), (1, 0))):
        both = spread(came_ref[holder, place + core])
        for side in (0, 1):
            slot = 2 * w + side
            pairs.append(((high_ref[slot], low_ref[slot]), both[side]))

    total = own_ref[...] + dot3_sum(pairs)
    for h in range(2):
        total_s[h] = total[:, 128 * h : 128 * h + 128]
    first = lanes((32, 128)) < 64
    sources = []
    for source in range(16):
        chip = source // 2
        packed = came_ref[source % 2, 4 + chip // 2, 32 * (chip % 2) : 32 * (chip % 2) + 32, :]
        turned = pltpu.roll(packed, 64, 1)
        sources += [jnp.where(first, packed, turned), jnp.where(first, turned, packed)]
    sources = split(jnp.concatenate(sources, axis=0))
    far = dot3k((second_ref[0:64], second_ref[64:128]), sources)
    first = lanes((16, 128)) < 64
    for t in range(4):
        for h in range(2):
            a = total_s[h, pl.ds(2 * t, 16, stride=8), :]
            b = total_s[h, pl.ds(2 * t + 1, 16, stride=8), :]
            local_s[t, pl.ds(2 * h, 16, stride=4), :] = jnp.where(first, a, pltpu.roll(b, 64, 1))
            local_s[t, pl.ds(2 * h + 1, 16, stride=4), :] = jnp.where(first, pltpu.roll(a, 64, 1), b)
    local = jnp.concatenate([local_s[t] for t in range(4)], axis=1)
    for c in range(4):
        far_s[pl.ds(c, 16, stride=4), :] = far[16 * c : 16 * c + 16]
    far = far_s[...]
    operators = split(l2l_ref[...].reshape(512, 64))
    lowered = dot3k(operators, split(far))
    first = lanes((64, 128)) < 64
    wide = [jnp.where(first, lowered[128 * t : 128 * t + 64], lowered[128 * t + 64 : 128 * t + 128]) for t in range(4)]
    place = 8 * (rows((512, 512)) % 64) + rows((512, 512)) // 64
    order = jnp.where(place == lanes((512, 512)), 1.0, 0.0).astype(BF16)
    head, tail = split(jnp.concatenate(wide, axis=1))
    local = local + dot(jnp.concatenate([head, tail], axis=1), jnp.concatenate([order, order], axis=0))
    out_ref[...] = dot3k(operators, split(local)).reshape(8, 64, 512)


SMEM = pl.BlockSpec(memory_space=pltpu.SMEM)
VMEM = pl.BlockSpec(memory_space=pltpu.VMEM)
HBM = pl.BlockSpec(memory_space=pltpu.HBM)
LIMIT = pltpu.CompilerParams(vmem_limit_bytes=24 * 1024 * 1024)


def in_hbm(x):
    return pltpu.with_memory_space_constraint(x, pltpu.HBM)


def upward(leaf_multipoles, m2m_ops, m2l_ops, send_blocks, send_counts, list1_src, list1_pat, list2_src, list2_pat):
    patterns = m2l_ops.shape[0]
    lists = [x[0, 0] for x in (list1_src, list1_pat, list2_src, list2_pat)]
    return pl.pallas_call(
        upward_kernel,
        out_shape=[
            jax.ShapeDtypeStruct((64, 512), F32),
            jax.ShapeDtypeStruct((4, 64, 128), F32),
            pltpu.HBM((8, 32, 128), F32),
            jax.ShapeDtypeStruct((144, patterns), BF16),
            jax.ShapeDtypeStruct((EARLY, 128, 256), F32),
            jax.ShapeDtypeStruct((2, 16 * EARLY, 128), F32),
        ],
        in_specs=[HBM] * 9,
        out_specs=[VMEM, VMEM, HBM, VMEM, VMEM, VMEM],
        scratch_shapes=[
            pltpu.SMEM((1, 1, 2, 4), jnp.int32),
            pltpu.SMEM((1, 1, 4), jnp.int32),
            pltpu.VMEM((8, 64, 512), F32),
            pltpu.VMEM((8, 64, 64), F32),
            *[pltpu.VMEM(x.shape, jnp.int32) for x in lists],
            pltpu.VMEM((4 * EARLY, 64, patterns), F32),
            pltpu.VMEM((64, 512), F32),
            pltpu.VMEM((512, 128), F32),
            pltpu.VMEM((64, 512), F32),
            pltpu.VMEM((8, 64, 128), F32),
            pltpu.VMEM((8, 32, 128), F32),
            pltpu.SemaphoreType.DMA((11,)),
        ],
        compiler_params=LIMIT,
        cost_estimate=pl.CostEstimate(flops=10**9, bytes_accessed=12 * 10**6, transcendentals=0),
        name="upward",
    )(
        in_hbm(jnp.transpose(send_blocks, (0, 1, 3, 2))),
        in_hbm(send_counts),
        in_hbm(leaf_multipoles),
        in_hbm(m2m_ops),
        *[in_hbm(x) for x in lists],
        in_hbm(jnp.transpose(m2l_ops, (1, 2, 0))),
    )


def weights(picks, table, early, m2l_ops, level1):
    patterns = m2l_ops.shape[0]
    return pl.pallas_call(
        weights_kernel,
        out_shape=[
            jax.ShapeDtypeStruct((8, 128, 256), BF16),
            jax.ShapeDtypeStruct((8, 128, 256), BF16),
            jax.ShapeDtypeStruct((128, 256), F32),
            jax.ShapeDtypeStruct((128, 1024), BF16),
        ],
        in_specs=[VMEM] * 3 + [HBM] + [VMEM],
        out_specs=[VMEM] * 4,
        scratch_shapes=[
            pltpu.VMEM((16 - EARLY, 128, 256), F32),
            pltpu.VMEM((2, 256 - 16 * EARLY, 128), F32),
            pltpu.VMEM((64 - 4 * EARLY, 64, patterns), F32),
            pltpu.SemaphoreType.DMA,
        ],
        compiler_params=LIMIT,
        name="weights",
    )(picks, table, early, in_hbm(jnp.transpose(m2l_ops, (1, 2, 0))), level1)


def downward(high, low, own, second, came, l2l_ops):
    return pl.pallas_call(
        downward_kernel,
        out_shape=jax.ShapeDtypeStruct((8, 64, 512), F32),
        in_specs=[VMEM] * 6,
        out_specs=VMEM,
        scratch_shapes=[pltpu.VMEM((2, 128, 128), F32), pltpu.VMEM((4, 64, 128), F32), pltpu.VMEM((64, 128), F32)],
        compiler_params=LIMIT,
        name="downward",
    )(high, low, own, second, came, l2l_ops)


def on_device(
    leaf_multipoles, m2m_ops, l2l_ops, m2l_ops, send_blocks, send_counts, list1_src, list1_pat, list2_src, list2_pat
):
    doms, inners = lax.axis_size("dom"), lax.axis_size("inner")
    level1, sends, level2, picks, table, early = upward(
        leaf_multipoles, m2m_ops, m2l_ops, send_blocks, send_counts, list1_src, list1_pat, list2_src, list2_pat
    )
    core = lax.axis_index("inner") % 2
    cores = [[2 * x, 2 * x + 1] for x in range(inners // 2)]

    def routed(block, side):
        route = []
        for d in range(doms):
            for i in range(inners):
                to = d + side * (1 + i % 2)
                if 0 <= to < doms:
                    route.append((d * inners + i, to * inners + i))
        return lax.ppermute(block, ("dom", "inner"), route)

    def both_cores(block):
        return lax.all_gather(block, "inner", axis=0, axis_index_groups=cores)

    chips = [[2 * x + c for x in range(inners // 2)] for c in range(2)]
    own_side = lax.all_to_all(level2, "inner", 0, 0, axis_index_groups=chips)
    chip_sends = both_cores(sends)
    upper = lax.dynamic_index_in_dim(chip_sends, 2 + core, 1, keepdims=False)
    lower = lax.dynamic_index_in_dim(chip_sends, 1 - core, 1, keepdims=False)
    came_up = routed(upper, 1)
    came_down = routed(lower, -1)
    operators = weights(picks, table, early, m2l_ops, level1)
    came = jnp.concatenate([came_down, came_up, own_side.reshape(4, 64, 128)], axis=0)
    return downward(*operators, both_cores(came), l2l_ops)


def solution(mesh):
    placed = (
        P(None, None, ("dom", "inner")),
        P(),
        P(),
        P(),
        P("dom", "inner", None, None),
        P("dom", "inner", None),
        P("dom", "inner", None, None),
        P("dom", "inner", None, None),
        P("dom", "inner", None, None),
        P("dom", "inner", None, None),
    )
    return jax.shard_map(
        on_device,
        mesh=mesh,
        in_specs=placed,
        out_specs=P(None, None, ("dom", "inner")),
        check_vma=False,
    )
```

```python
import jax
import jax.numpy as jnp
from jax import lax
from jax.experimental import pallas as pl
from jax.experimental.pallas import tpu as pltpu
from jax.sharding import PartitionSpec as P

F32 = jnp.float32
BF16 = jnp.bfloat16
NT = (((1,), (1,)), ((), ()))


def split(x):
    high = x.astype(BF16)
    return high, (x - high.astype(F32)).astype(BF16)


def dot(a, b):
    return jnp.dot(a, b, preferred_element_type=F32)


def dot_nt(a, b):
    return lax.dot_general(a, b, NT, preferred_element_type=F32)


def dot3(a, b, product=dot):
    n = a[0].shape[0]
    both = product(jnp.concatenate(a, axis=0), b[0])
    return both[:n] + (product(a[0], b[1]) + both[n:])


def dot3_sum(pairs):
    left = [x for a, _ in pairs for x in (a[0], a[0], a[1])]
    right = [x for _, b in pairs for x in (b[0], b[1], b[0])]
    return dot(jnp.concatenate(left, axis=1), jnp.concatenate(right, axis=0))


def dot3k(a, b):
    return dot3_sum([(a, b)])


def lanes(shape):
    return lax.broadcasted_iota(jnp.int32, shape, len(shape) - 1)


def rows(shape):
    return lax.broadcasted_iota(jnp.int32, shape, len(shape) - 2)


def four_blocks(low, high):
    none = jnp.zeros_like(low)
    left = jnp.concatenate([low, high, none, none], axis=0)
    right = jnp.concatenate([none, none, low, high], axis=0)
    return jnp.concatenate([left, right], axis=1)


def spread(pair):
    first = lanes(pair.shape) < 64
    turned = pltpu.roll(pair, 64, 1)
    result = []
    for side in (0, 1):
        low, high = (pair, turned) if side == 0 else (turned, pair)
        low = split(jnp.where(first, low, 0.0))
        high = split(jnp.where(first, 0.0, high))
        result.append((four_blocks(low[0], high[0]), four_blocks(low[1], high[1])))
    return result


EARLY = 4


def translate(picks, m2l_ref, table_ref, second_ref):
    for g in range(m2l_ref.shape[0] // 4):
        high, low = split(m2l_ref[4 * g : 4 * g + 4].reshape(256, m2l_ref.shape[2]))
        operators = dot_nt(jnp.concatenate([picks, picks], axis=1), jnp.concatenate([high, low], axis=1))
        table_ref[g] = operators[0:128]
        for h in range(2):
            second_ref[h, 16 * g : 16 * g + 16, :] = operators[128:144, 128 * h : 128 * h + 128]


def upward_kernel(
    blocks_hbm, counts_hbm, leaf_hbm, m2m_hbm, src_hbm, pat_hbm, src2_hbm, pat2_hbm, m2l_hbm,
    level1_ref, sends_ref, level2_hbm, picks_ref, table_ref, second_ref,
    blocks, counts, leaf, m2m, src_ref, pat_ref, src2_ref, pat2_ref, m2l_ref, ops, turned, grouped, twice, copies, sems
):
    def copy(source, target, k):
        return pltpu.make_async_copy(source, target, sems.at[k])

    first_copies = [
        copy(m2m_hbm, m2m, 0),
        copy(leaf_hbm.at[0:4], leaf.at[0:4], 1),
        copy(leaf_hbm.at[4:8], leaf.at[4:8], 2),
        copy(blocks_hbm, blocks, 3),
        copy(counts_hbm, counts, 4),
    ]
    list_copies = [
        copy(src_hbm, src_ref, 5), copy(pat_hbm, pat_ref, 6), copy(src2_hbm, src2_ref, 7), copy(pat2_hbm, pat2_ref, 8)
    ]
    m2l_copy = copy(m2l_hbm.at[0 : 4 * EARLY], m2l_ref, 10)
    for c in first_copies + list_copies + [m2l_copy]:
        c.start()
    first_copies[0].wait()
    for o in range(8):
        ops[:, o * 64 : (o + 1) * 64] = m2m[o]
    operators = split(ops[...])
    level1 = jnp.zeros((64, 512), F32)
    for half in range(2):
        first_copies[1 + half].wait()
        operator = [part[:, 256 * half : 256 * half + 256] for part in operators]
        level1 = level1 + dot3(operator, split(leaf[4 * half : 4 * half + 4].reshape(256, 512)))
    level1_ref[...] = level1
    turned[...] = jnp.concatenate([level1, level1], axis=0).T
    for o in range(8):
        grouped[:, o * 64 : (o + 1) * 64] = turned[pl.ds(o, 64, stride=8), :][:, 0:64]
    level2 = dot3(operators, split(grouped[...]), dot_nt)
    first = lanes((32, 128)) < 64
    wide = jnp.concatenate([level2, level2], axis=1)
    packed = jnp.where(first, wide[0:32], wide[32:64])
    for member in range(8):
        copies[member] = packed
    level2_copy = copy(copies, level2_hbm, 9)
    level2_copy.start()
    first = lanes((64, 128)) < 64
    for t in range(4):
        tile = level1[:, t * 128 : (t + 1) * 128]
        other = pltpu.roll(tile, 64, 1)
        twice[2 * t] = jnp.where(first, tile, other)
        twice[2 * t + 1] = jnp.where(first, other, tile)
    first_copies[3].wait()
    first_copies[4].wait()
    for w in range(4):
        count = counts[0, 0, w]
        left = jnp.where(count > 0, twice[blocks[0, 0, 0, w]], 0.0)
        right = jnp.where(count > 1, twice[blocks[0, 0, 1, w]], 0.0)
        sends_ref[w] = jnp.where(first, left, right)
    for c in list_copies:
        c.wait()
    patterns = m2l_ref.shape[2]
    entries = src_ref.shape[1]
    code = src_ref[...] * 8 + rows((8, entries))
    pat = pat_ref[...]
    tally = jnp.zeros((128, patterns), F32)
    for r in range(8):
        sources = jnp.where(code[r : r + 1] == rows((128, entries)), 1.0, 0.0).astype(BF16)
        kinds = jnp.where(pat[r : r + 1] == rows((patterns, entries)), 1.0, 0.0).astype(BF16)
        tally = tally + dot_nt(sources, kinds)
    entries = src2_ref.shape[1]
    sources = jnp.where(src2_ref[...] == rows((16, entries)), 1.0, 0.0).astype(BF16)
    kinds = jnp.where(pat2_ref[...] == rows((patterns, entries)), 1.0, 0.0).astype(BF16)
    picks = jnp.concatenate([tally, dot_nt(sources, kinds)], axis=0).astype(BF16)
    picks_ref[...] = picks
    m2l_copy.wait()
    translate(picks, m2l_ref, table_ref, second_ref)
    level2_copy.wait()


def weights_kernel(
    picks_ref, table_ref, early_ref, m2l_hbm, level1_ref, high_ref, low_ref, own_ref, second_ref,
    table, second_s, m2l_ref, sem
):
    m2l_copy = pltpu.make_async_copy(m2l_hbm.at[4 * EARLY : 64], m2l_ref, sem)
    m2l_copy.start()
    m2l_copy.wait()
    translate(picks_ref[...], m2l_ref, table, second_s)

    def operators(s):
        place = pl.ds(8 * s, 8)
        return split(jnp.concatenate([table_ref[:, place, :], table[:, place, :]], axis=0).reshape(128, 256))

    for s in range(8, 16):
        high_ref[s - 8], low_ref[s - 8] = operators(s)
    first = lanes((16, 128)) < 64
    for t in range(8):
        parts = []
        for h in range(2):
            a, b = (
                jnp.concatenate([ref[h, pl.ds(s, ref.shape[1] // 16, stride=16), :] for ref in (early_ref, second_s)], axis=0)
                for s in (2 * t, 2 * t + 1)
            )
            parts.append(jnp.where(first, a, pltpu.roll(b, 64, 1)))
            parts.append(jnp.where(first, pltpu.roll(a, 64, 1), b))
        second_ref[:, 128 * t : 128 * t + 128] = jnp.concatenate(split(jnp.concatenate(parts, axis=0)), axis=0)
    total = jnp.zeros((128, 256), F32)
    for t in range(4):
        both = spread(level1_ref[:, t * 128 : (t + 1) * 128])
        for side in (0, 1):
            total = total + dot3(operators(2 * t + side), both[side])
    own_ref[...] = total


def downward_kernel(
    high_ref, low_ref, own_ref, second_ref, came_ref, l2l_ref, out_ref, total_s, local_s, far_s
):
    pairs = []
    core = lax.axis_index("inner") % 2
    dom = lax.axis_index("dom")
    for w, (holder, above) in enumerate(((1, 0), (0, 0), (0, 1), (1, 1))):
        first_up = 1 - (dom >> holder) % 2
        phase = (first_up + above) % 2
        both = spread(came_ref[holder, 2 * phase + core])
        for side in (0, 1):
            slot = 2 * w + side
            pairs.append(((high_ref[slot], low_ref[slot]), both[side]))

    total = own_ref[...] + dot3_sum(pairs)
    for h in range(2):
        total_s[h] = total[:, 128 * h : 128 * h + 128]
    first = lanes((32, 128)) < 64
    sources = []
    for source in range(16):
        chip = source // 2
        packed = came_ref[source % 2, 4 + chip // 2, 32 * (chip % 2) : 32 * (chip % 2) + 32, :]
        turned = pltpu.roll(packed, 64, 1)
        sources += [jnp.where(first, packed, turned), jnp.where(first, turned, packed)]
    sources = split(jnp.concatenate(sources, axis=0))
    far = dot3k((second_ref[0:64], second_ref[64:128]), sources)
    first = lanes((16, 128)) < 64
    for t in range(4):
        for h in range(2):
            a = total_s[h, pl.ds(2 * t, 16, stride=8), :]
            b = total_s[h, pl.ds(2 * t + 1, 16, stride=8), :]
            local_s[t, pl.ds(2 * h, 16, stride=4), :] = jnp.where(first, a, pltpu.roll(b, 64, 1))
            local_s[t, pl.ds(2 * h + 1, 16, stride=4), :] = jnp.where(first, pltpu.roll(a, 64, 1), b)
    local = jnp.concatenate([local_s[t] for t in range(4)], axis=1)
    for c in range(4):
        far_s[pl.ds(c, 16, stride=4), :] = far[16 * c : 16 * c + 16]
    far = far_s[...]
    operators = split(l2l_ref[...].reshape(512, 64))
    lowered = dot3k(operators, split(far))
    first = lanes((64, 128)) < 64
    wide = [jnp.where(first, lowered[128 * t : 128 * t + 64], lowered[128 * t + 64 : 128 * t + 128]) for t in range(4)]
    place = 8 * (rows((512, 512)) % 64) + rows((512, 512)) // 64
    order = jnp.where(place == lanes((512, 512)), 1.0, 0.0).astype(BF16)
    head, tail = split(jnp.concatenate(wide, axis=1))
    local = local + dot(jnp.concatenate([head, tail], axis=1), jnp.concatenate([order, order], axis=0))
    out_ref[...] = dot3k(operators, split(local)).reshape(8, 64, 512)


SMEM = pl.BlockSpec(memory_space=pltpu.SMEM)
VMEM = pl.BlockSpec(memory_space=pltpu.VMEM)
HBM = pl.BlockSpec(memory_space=pltpu.HBM)
LIMIT = pltpu.CompilerParams(vmem_limit_bytes=24 * 1024 * 1024)


def in_hbm(x):
    return pltpu.with_memory_space_constraint(x, pltpu.HBM)


def upward(leaf_multipoles, m2m_ops, m2l_ops, send_blocks, send_counts, list1_src, list1_pat, list2_src, list2_pat):
    patterns = m2l_ops.shape[0]
    lists = [x[0, 0] for x in (list1_src, list1_pat, list2_src, list2_pat)]
    return pl.pallas_call(
        upward_kernel,
        out_shape=[
            jax.ShapeDtypeStruct((64, 512), F32),
            jax.ShapeDtypeStruct((4, 64, 128), F32),
            pltpu.HBM((8, 32, 128), F32),
            jax.ShapeDtypeStruct((144, patterns), BF16),
            jax.ShapeDtypeStruct((EARLY, 128, 256), F32),
            jax.ShapeDtypeStruct((2, 16 * EARLY, 128), F32),
        ],
        in_specs=[HBM] * 9,
        out_specs=[VMEM, VMEM, HBM, VMEM, VMEM, VMEM],
        scratch_shapes=[
            pltpu.SMEM((1, 1, 2, 4), jnp.int32),
            pltpu.SMEM((1, 1, 4), jnp.int32),
            pltpu.VMEM((8, 64, 512), F32),
            pltpu.VMEM((8, 64, 64), F32),
            *[pltpu.VMEM(x.shape, jnp.int32) for x in lists],
            pltpu.VMEM((4 * EARLY, 64, patterns), F32),
            pltpu.VMEM((64, 512), F32),
            pltpu.VMEM((512, 128), F32),
            pltpu.VMEM((64, 512), F32),
            pltpu.VMEM((8, 64, 128), F32),
            pltpu.VMEM((8, 32, 128), F32),
            pltpu.SemaphoreType.DMA((11,)),
        ],
        compiler_params=LIMIT,
        cost_estimate=pl.CostEstimate(flops=10**9, bytes_accessed=12 * 10**6, transcendentals=0),
        name="upward",
    )(
        in_hbm(jnp.transpose(send_blocks, (0, 1, 3, 2))),
        in_hbm(send_counts),
        in_hbm(leaf_multipoles),
        in_hbm(m2m_ops),
        *[in_hbm(x) for x in lists],
        in_hbm(jnp.transpose(m2l_ops, (1, 2, 0))),
    )


def weights(picks, table, early, m2l_ops, level1):
    patterns = m2l_ops.shape[0]
    return pl.pallas_call(
        weights_kernel,
        out_shape=[
            jax.ShapeDtypeStruct((8, 128, 256), BF16),
            jax.ShapeDtypeStruct((8, 128, 256), BF16),
            jax.ShapeDtypeStruct((128, 256), F32),
            jax.ShapeDtypeStruct((128, 1024), BF16),
        ],
        in_specs=[VMEM] * 3 + [HBM] + [VMEM],
        out_specs=[VMEM] * 4,
        scratch_shapes=[
            pltpu.VMEM((16 - EARLY, 128, 256), F32),
            pltpu.VMEM((2, 256 - 16 * EARLY, 128), F32),
            pltpu.VMEM((64 - 4 * EARLY, 64, patterns), F32),
            pltpu.SemaphoreType.DMA,
        ],
        compiler_params=LIMIT,
        name="weights",
    )(picks, table, early, in_hbm(jnp.transpose(m2l_ops, (1, 2, 0))), level1)


def downward(high, low, own, second, came, l2l_ops):
    return pl.pallas_call(
        downward_kernel,
        out_shape=jax.ShapeDtypeStruct((8, 64, 512), F32),
        in_specs=[VMEM] * 6,
        out_specs=VMEM,
        scratch_shapes=[pltpu.VMEM((2, 128, 128), F32), pltpu.VMEM((4, 64, 128), F32), pltpu.VMEM((64, 128), F32)],
        compiler_params=LIMIT,
        name="downward",
    )(high, low, own, second, came, l2l_ops)


def on_device(
    leaf_multipoles, m2m_ops, l2l_ops, m2l_ops, send_blocks, send_counts, list1_src, list1_pat, list2_src, list2_pat
):
    doms, inners = lax.axis_size("dom"), lax.axis_size("inner")
    level1, sends, level2, picks, table, early = upward(
        leaf_multipoles, m2m_ops, m2l_ops, send_blocks, send_counts, list1_src, list1_pat, list2_src, list2_pat
    )
    core = lax.axis_index("inner") % 2
    cores = [[2 * x, 2 * x + 1] for x in range(inners // 2)]

    first_up = (lax.axis_index("dom") >> core) % 2 == 0

    def swapped(block, phase):
        route = []
        for d in range(doms):
            for i in range(inners):
                away = 1 + i % 2
                to = d + away if d // away % 2 == phase else d - away
                if 0 <= to < doms:
                    route.append((d * inners + i, to * inners + i))
        return lax.ppermute(block, ("dom", "inner"), route)

    def both_cores(block):
        return lax.all_gather(block, "inner", axis=0, axis_index_groups=cores)

    chips = [[2 * x + c for x in range(inners // 2)] for c in range(2)]
    own_side = lax.all_to_all(level2, "inner", 0, 0, axis_index_groups=chips)
    chip_sends = both_cores(sends)
    to_up, to_down = 2 + core, 1 - core
    first = lax.dynamic_index_in_dim(chip_sends, jnp.where(first_up, to_up, to_down), 1, keepdims=False)
    second = lax.dynamic_index_in_dim(chip_sends, jnp.where(first_up, to_down, to_up), 1, keepdims=False)
    came_first = swapped(first, 0)
    came_second = swapped(second, 1)
    operators = weights(picks, table, early, m2l_ops, level1)
    came = jnp.concatenate([came_first, came_second, own_side.reshape(4, 64, 128)], axis=0)
    return downward(*operators, both_cores(came), l2l_ops)


def solution(mesh):
    placed = (
        P(None, None, ("dom", "inner")),
        P(),
        P(),
        P(),
        P("dom", "inner", None, None),
        P("dom", "inner", None),
        P("dom", "inner", None, None),
        P("dom", "inner", None, None),
        P("dom", "inner", None, None),
        P("dom", "inner", None, None),
    )
    return jax.shard_map(
        on_device,
        mesh=mesh,
        in_specs=placed,
        out_specs=P(None, None, ("dom", "inner")),
        check_vma=False,
    )
```

```python
import jax
import jax.numpy as jnp
from jax import lax
from jax.experimental import pallas as pl
from jax.experimental.pallas import tpu as pltpu
from jax.sharding import PartitionSpec as P

F32 = jnp.float32
BF16 = jnp.bfloat16
NT = (((1,), (1,)), ((), ()))


def split(x):
    high = x.astype(BF16)
    return high, (x - high.astype(F32)).astype(BF16)


def dot(a, b):
    return jnp.dot(a, b, preferred_element_type=F32)


def dot_nt(a, b):
    return lax.dot_general(a, b, NT, preferred_element_type=F32)


def dot3(a, b, product=dot):
    n = a[0].shape[0]
    both = product(jnp.concatenate(a, axis=0), b[0])
    return both[:n] + (product(a[0], b[1]) + both[n:])


def dot3_sum(pairs):
    left = [x for a, _ in pairs for x in (a[0], a[0], a[1])]
    right = [x for _, b in pairs for x in (b[0], b[1], b[0])]
    return dot(jnp.concatenate(left, axis=1), jnp.concatenate(right, axis=0))


def dot3k(a, b):
    return dot3_sum([(a, b)])


def lanes(shape):
    return lax.broadcasted_iota(jnp.int32, shape, len(shape) - 1)


def rows(shape):
    return lax.broadcasted_iota(jnp.int32, shape, len(shape) - 2)


def four_blocks(low, high):
    none = jnp.zeros_like(low)
    left = jnp.concatenate([low, high, none, none], axis=0)
    right = jnp.concatenate([none, none, low, high], axis=0)
    return jnp.concatenate([left, right], axis=1)


def spread(pair):
    first = lanes(pair.shape) < 64
    turned = pltpu.roll(pair, 64, 1)
    result = []
    for side in (0, 1):
        low, high = (pair, turned) if side == 0 else (turned, pair)
        low = split(jnp.where(first, low, 0.0))
        high = split(jnp.where(first, 0.0, high))
        result.append((four_blocks(low[0], high[0]), four_blocks(low[1], high[1])))
    return result


def upward_kernel(
    blocks_hbm, counts_hbm, leaf_hbm, m2m_hbm, level1_ref, sends_ref, level2_ref,
    blocks, counts, leaf, m2m, ops, turned, grouped, twice, sems
):
    def copy(source, target, k):
        return pltpu.make_async_copy(source, target, sems.at[k])

    first_copies = [
        copy(m2m_hbm, m2m, 0),
        copy(leaf_hbm.at[0:4], leaf.at[0:4], 1),
        copy(leaf_hbm.at[4:8], leaf.at[4:8], 2),
        copy(blocks_hbm, blocks, 3),
        copy(counts_hbm, counts, 4),
    ]
    for c in first_copies:
        c.start()
    first_copies[0].wait()
    for o in range(8):
        ops[:, o * 64 : (o + 1) * 64] = m2m[o]
    operators = split(ops[...])
    level1 = jnp.zeros((64, 512), F32)
    for half in range(2):
        first_copies[1 + half].wait()
        operator = [part[:, 256 * half : 256 * half + 256] for part in operators]
        level1 = level1 + dot3(operator, split(leaf[4 * half : 4 * half + 4].reshape(256, 512)))
    level1_ref[...] = level1
    turned[...] = jnp.concatenate([level1, level1], axis=0).T
    for o in range(8):
        grouped[:, o * 64 : (o + 1) * 64] = turned[pl.ds(o, 64, stride=8), :][:, 0:64]
    level2 = dot3(operators, split(grouped[...]), dot_nt)
    first = lanes((32, 128)) < 64
    wide = jnp.concatenate([level2, level2], axis=1)
    packed = jnp.where(first, wide[0:32], wide[32:64])
    for member in range(8):
        level2_ref[member] = packed
    first = lanes((64, 128)) < 64
    for t in range(4):
        tile = level1[:, t * 128 : (t + 1) * 128]
        other = pltpu.roll(tile, 64, 1)
        twice[2 * t] = jnp.where(first, tile, other)
        twice[2 * t + 1] = jnp.where(first, other, tile)
    first_copies[3].wait()
    first_copies[4].wait()
    for w in range(4):
        count = counts[0, 0, w]
        left = jnp.where(count > 0, twice[blocks[0, 0, 0, w]], 0.0)
        right = jnp.where(count > 1, twice[blocks[0, 0, 1, w]], 0.0)
        sends_ref[w] = jnp.where(first, left, right)


def weights_kernel(
    src_ref, pat_ref, src2_ref, pat2_ref, m2l_hbm, level1_ref, high_ref, low_ref, own_ref, second_ref, table, second_s, m2l_ref, sems
):
    patterns = m2l_ref.shape[2]
    copies = [
        [
            pltpu.make_async_copy(m2l_hbm.at[part], m2l_ref.at[part], sems.at[4 * quarter + c])
            for c in range(4)
            for part in [pl.ds(16 * c + 4 * quarter, 4)]
        ]
        for quarter in range(4)
    ]
    for quarter in copies:
        for c in quarter:
            c.start()
    entries = src_ref.shape[1]
    code = src_ref[...] * 8 + rows((8, entries))
    pat = pat_ref[...]
    tally = jnp.zeros((128, patterns), F32)
    for r in range(8):
        sources = jnp.where(code[r : r + 1] == rows((128, entries)), 1.0, 0.0).astype(BF16)
        kinds = jnp.where(pat[r : r + 1] == rows((patterns, entries)), 1.0, 0.0).astype(BF16)
        tally = tally + dot_nt(sources, kinds)
    entries = src2_ref.shape[1]
    sources = jnp.where(src2_ref[...] == rows((16, entries)), 1.0, 0.0).astype(BF16)
    kinds = jnp.where(pat2_ref[...] == rows((patterns, entries)), 1.0, 0.0).astype(BF16)
    picks = jnp.concatenate([tally, dot_nt(sources, kinds)], axis=0).astype(BF16)
    for g in range(16):
        if g % 4 == 0:
            for c in copies[g // 4]:
                c.wait()
        high, low = split(jnp.concatenate([m2l_ref[16 * c + g] for c in range(4)], axis=0))
        operators = dot_nt(picks, high) + dot_nt(picks, low)
        table[g] = operators[0:128]
        for h in range(2):
            second_s[h, 16 * g : 16 * g + 16, :] = operators[128:144, 128 * h : 128 * h + 128]
    for s in range(8, 16):
        high, low = split(table[:, 8 * s : 8 * s + 8, :].reshape(128, 256))
        high_ref[s - 8] = high
        low_ref[s - 8] = low
    first = lanes((16, 128)) < 64
    for t in range(8):
        parts = []
        for h in range(2):
            a = second_s[h, pl.ds(2 * t, 16, stride=16), :]
            b = second_s[h, pl.ds(2 * t + 1, 16, stride=16), :]
            parts.append(jnp.where(first, a, pltpu.roll(b, 64, 1)))
            parts.append(jnp.where(first, pltpu.roll(a, 64, 1), b))
        second_ref[:, 128 * t : 128 * t + 128] = jnp.concatenate(split(jnp.concatenate(parts, axis=0)), axis=0)
    total = jnp.zeros((128, 256), F32)
    for t in range(4):
        both = spread(level1_ref[:, t * 128 : (t + 1) * 128])
        for side in (0, 1):
            s = 2 * t + side
            total = total + dot3(split(table[:, 8 * s : 8 * s + 8, :].reshape(128, 256)), both[side])
    own_ref[...] = total


def downward_kernel(
    high_ref, low_ref, own_ref, second_ref, came_ref, l2l_ref, out_ref, total_s
):
    pairs = []
    core = lax.axis_index("inner") % 2
    dom = lax.axis_index("dom")
    for w, (holder, above) in enumerate(((1, 0), (0, 0), (0, 1), (1, 1))):
        first_up = 1 - (dom >> holder) % 2
        phase = (first_up + above) % 2
        both = spread(came_ref[holder, 2 * (1 - phase) + core])
        for side in (0, 1):
            slot = 2 * w + side
            pairs.append(((high_ref[slot], low_ref[slot]), both[side]))

    total = own_ref[...] + dot3_sum(pairs)
    for h in range(2):
        total_s[h] = total[:, 128 * h : 128 * h + 128]
    first = lanes((32, 128)) < 64
    sources = []
    for source in range(16):
        chip = source // 2
        packed = came_ref[source % 2, 4 + chip // 2, 32 * (chip % 2) : 32 * (chip % 2) + 32, :]
        turned = pltpu.roll(packed, 64, 1)
        sources += [jnp.where(first, packed, turned), jnp.where(first, turned, packed)]
    sources = split(jnp.concatenate(sources, axis=0))
    far = dot3k((second_ref[0:64], second_ref[64:128]), sources)
    first = lanes((16, 128)) < 64
    local = []
    for t in range(4):
        parts = []
        for h in range(2):
            a = total_s[h, pl.ds(2 * t, 16, stride=8), :]
            b = total_s[h, pl.ds(2 * t + 1, 16, stride=8), :]
            parts.append(jnp.where(first, a, pltpu.roll(b, 64, 1)))
            parts.append(jnp.where(first, pltpu.roll(a, 64, 1), b))
        local.append(jnp.concatenate(parts, axis=0))
    local = jnp.concatenate(local, axis=1)
    operators = split(l2l_ref[...].reshape(512, 64))
    lowered = dot3k(operators, split(far))
    first = lanes((64, 128)) < 64
    wide = [jnp.where(first, lowered[128 * t : 128 * t + 64], lowered[128 * t + 64 : 128 * t + 128]) for t in range(4)]
    place = 8 * (rows((512, 512)) % 64) + rows((512, 512)) // 64
    order = jnp.where(place == lanes((512, 512)), 1.0, 0.0).astype(BF16)
    head, tail = split(jnp.concatenate(wide, axis=1))
    local = local + dot(jnp.concatenate([head, tail], axis=1), jnp.concatenate([order, order], axis=0))
    out_ref[...] = dot3k(operators, split(local)).reshape(8, 64, 512)


SMEM = pl.BlockSpec(memory_space=pltpu.SMEM)
VMEM = pl.BlockSpec(memory_space=pltpu.VMEM)
HBM = pl.BlockSpec(memory_space=pltpu.HBM)
LIMIT = pltpu.CompilerParams(vmem_limit_bytes=24 * 1024 * 1024)


def in_hbm(x):
    return pltpu.with_memory_space_constraint(x, pltpu.HBM)


def upward(leaf_multipoles, m2m_ops, send_blocks, send_counts):
    return pl.pallas_call(
        upward_kernel,
        out_shape=[
            jax.ShapeDtypeStruct((64, 512), F32),
            jax.ShapeDtypeStruct((4, 64, 128), F32),
            jax.ShapeDtypeStruct((8, 32, 128), F32),
        ],
        in_specs=[HBM] * 4,
        out_specs=[VMEM] * 3,
        scratch_shapes=[
            pltpu.SMEM((1, 1, 2, 4), jnp.int32),
            pltpu.SMEM((1, 1, 4), jnp.int32),
            pltpu.VMEM((8, 64, 512), F32),
            pltpu.VMEM((8, 64, 64), F32),
            pltpu.VMEM((64, 512), F32),
            pltpu.VMEM((512, 128), F32),
            pltpu.VMEM((64, 512), F32),
            pltpu.VMEM((8, 64, 128), F32),
            pltpu.SemaphoreType.DMA((5,)),
        ],
        compiler_params=LIMIT,
        cost_estimate=pl.CostEstimate(flops=10**9, bytes_accessed=12 * 10**6, transcendentals=0),
        name="upward",
    )(
        in_hbm(jnp.transpose(send_blocks, (0, 1, 3, 2))),
        in_hbm(send_counts),
        in_hbm(leaf_multipoles),
        in_hbm(m2m_ops),
    )


def weights(list1_src, list1_pat, list2_src, list2_pat, m2l_ops, level1):
    patterns = m2l_ops.shape[0]
    return pl.pallas_call(
        weights_kernel,
        out_shape=[
            jax.ShapeDtypeStruct((8, 128, 256), BF16),
            jax.ShapeDtypeStruct((8, 128, 256), BF16),
            jax.ShapeDtypeStruct((128, 256), F32),
            jax.ShapeDtypeStruct((128, 1024), BF16),
        ],
        in_specs=[VMEM] * 4 + [HBM] + [VMEM],
        out_specs=[VMEM] * 4,
        scratch_shapes=[
            pltpu.VMEM((16, 128, 256), F32),
            pltpu.VMEM((2, 256, 128), F32),
            pltpu.VMEM((64, 64, patterns), F32),
            pltpu.SemaphoreType.DMA((16,)),
        ],
        compiler_params=LIMIT,
        name="weights",
    )(
        list1_src[0, 0],
        list1_pat[0, 0],
        list2_src[0, 0],
        list2_pat[0, 0],
        in_hbm(jnp.transpose(m2l_ops, (1, 2, 0))),
        level1,
    )


def downward(high, low, own, second, came, l2l_ops):
    return pl.pallas_call(
        downward_kernel,
        out_shape=jax.ShapeDtypeStruct((8, 64, 512), F32),
        in_specs=[VMEM] * 6,
        out_specs=VMEM,
        scratch_shapes=[pltpu.VMEM((2, 128, 128), F32)],
        compiler_params=LIMIT,
        name="downward",
    )(high, low, own, second, came, l2l_ops)


def on_device(
    leaf_multipoles, m2m_ops, l2l_ops, m2l_ops, send_blocks, send_counts, list1_src, list1_pat, list2_src, list2_pat
):
    doms, inners = lax.axis_size("dom"), lax.axis_size("inner")
    level1, sends, level2 = upward(leaf_multipoles, m2m_ops, send_blocks, send_counts)
    core = lax.axis_index("inner") % 2
    cores = [[2 * x, 2 * x + 1] for x in range(inners // 2)]

    first_up = (lax.axis_index("dom") >> core) % 2 == 0

    def swapped(block, phase):
        route = []
        for d in range(doms):
            for i in range(inners):
                away = 1 + i % 2
                to = d + away if d // away % 2 == phase else d - away
                if 0 <= to < doms:
                    route.append((d * inners + i, to * inners + i))
        return lax.ppermute(block, ("dom", "inner"), route)

    def both_cores(block):
        return lax.all_gather(block, "inner", axis=0, axis_index_groups=cores)

    chips = [[2 * x + c for x in range(inners // 2)] for c in range(2)]
    own_side = lax.all_to_all(level2, "inner", 0, 0, axis_index_groups=chips)
    chip_sends = both_cores(sends)
    to_up, to_down = 2 + core, 1 - core
    first = lax.dynamic_index_in_dim(chip_sends, jnp.where(first_up, to_up, to_down), 1, keepdims=False)
    second = lax.dynamic_index_in_dim(chip_sends, jnp.where(first_up, to_down, to_up), 1, keepdims=False)
    came_first = swapped(first, 0)
    came_second = swapped(second, 1)
    operators = weights(list1_src, list1_pat, list2_src, list2_pat, m2l_ops, level1)
    came = jnp.concatenate([came_second, came_first, own_side.reshape(4, 64, 128)], axis=0)
    return downward(*operators, both_cores(came), l2l_ops)


def solution(mesh):
    placed = (
        P(None, None, ("dom", "inner")),
        P(),
        P(),
        P(),
        P("dom", "inner", None, None),
        P("dom", "inner", None),
        P("dom", "inner", None, None),
        P("dom", "inner", None, None),
        P("dom", "inner", None, None),
        P("dom", "inner", None, None),
    )
    return jax.shard_map(
        on_device,
        mesh=mesh,
        in_specs=placed,
        out_specs=P(None, None, ("dom", "inner")),
        check_vma=False,
    )
```
